32 devices in a mesh: node: 8 (over y, x, core), local: 4 (over z).
Axes of the slice: x: 2, y: 2, z: 4, core: 2. Of those that a mesh axis runs over, the one named last changes fastest.
Arguments:
- moe_in: bfloat16 [512, 3584], P(('node', 'local')), may hold values from -6 to 6
- route_ids: int32 [512, 8], P(('node', 'local')), may hold values from 0 to 31, as said below
- route_weights: float32 [512, 8], P(('node', 'local')), may hold values from 0.05 to 0.6
- w_gate: bfloat16 [32, 3584, 1024], P(('node', 'local')), may hold values from -0.09375 to 0.09375
- w_up: bfloat16 [32, 3584, 1024], P(('node', 'local')), may hold values from -0.09375 to 0.09375
- w_down: bfloat16 [32, 1024, 3584], P(('node', 'local')), may hold values from -0.1875 to 0.1875
- queries: bfloat16 [32, 128, 576], P(('node', 'local')), may hold values from -70 to 70
- cache_latent: bfloat16 [32, 2048, 512], P(('node', 'local')), may hold values from -12 to 12
- cache_rope: bfloat16 [32, 64, 2048], P(('node', 'local')), may hold values from -2 to 2
- lengths: int32 [32], P(('node', 'local')), may hold values from 256 to 2048, as said below
Outputs:
- moe_out: bfloat16 [512, 3584], P(('node', 'local'))
- attn_out: bfloat16 [32, 128, 512], P(('node', 'local'))
The draws below stay inside these ranges and needn't reach their ends.
Inputs may be any that keep to these rules, and one draw needn't show every extreme that they name: `route_ids`: each row names 8 different experts, 2 in each of 4 different node groups; expert e lies in node group e // 4 and is held by the device of flat index e (node major). Within the rows of one device (aligned blocks of 16 rows) no node group is used by more than 16 rows and no expert is named by more than 8 rows; in every such block some node group is used by exactly 16 rows and each of its experts is named by exactly 8 rows. `lengths`: at least one row has all 2048 slots filled.
All inputs are finite; a program needn't handle non-finite values.
Results may differ from the reference program's by a relative error of at most 0.012.
Values may be sent and summed in bfloat16 or wider, within the bound.
A program may use at most 128 MiB of HBM per device.

```python
import math
import jax
import jax.numpy as jnp
from jax import lax

D = 3584
H = 1024
HEADS = 128
KV_RANK = 512
ROPE = 64
TOPK = 8
TOPG = 4
ROWS_DEV = 16
CACHE = 2048
GROUPS = 8
GROUP_EXPERTS = 4
EXPERTS = 32
SOURCES = 32
NODE_CAP = 16
TOKENS = 512
ATT_ROWS = 32


def draw_queries(key, part):
    key = jax.random.fold_in(key, 21)
    values = jnp.clip(0.5 * jax.random.normal(key, (ATT_ROWS, HEADS, KV_RANK + ROPE), jnp.float32), -3.0, 3.0)
    return values.astype(jnp.bfloat16)


def draw_cache_latent(key, part):
    key = jax.random.fold_in(key, 22)
    value_key, scale_key = jax.random.split(key)
    spread = jnp.exp(jax.random.uniform(scale_key, (ATT_ROWS, CACHE, 1), jnp.float32, jnp.log(0.3), jnp.log(3.0)))
    values = jnp.clip(jax.random.normal(value_key, (ATT_ROWS, CACHE, KV_RANK), jnp.float32), -4.0, 4.0) * spread
    return values.astype(jnp.bfloat16)


def draw_cache_rope(key, part):
    key = jax.random.fold_in(key, 23)
    values = jnp.clip(0.5 * jax.random.normal(key, (ATT_ROWS, ROPE, CACHE), jnp.float32), -2.0, 2.0)
    return values.astype(jnp.bfloat16)


def draw_lengths(key, part):
    key = jax.random.fold_in(key, 24)
    first_key, second_key = jax.random.split(key)
    drawn = jax.random.randint(first_key, (ATT_ROWS,), CACHE // 8, CACHE + 1, dtype=jnp.int32)
    full_row = jax.random.randint(second_key, (), 0, ATT_ROWS, dtype=jnp.int32)
    return jnp.where(jnp.arange(ATT_ROWS, dtype=jnp.int32) == full_row, CACHE, drawn).astype(jnp.int32)


def draw_route_ids(key, part):
    key = jax.random.fold_in(key, 25)
    keys = jax.random.split(key, 7)
    group_index = jnp.arange(GROUPS, dtype=jnp.int32)
    hot_group = jax.random.randint(keys[0], (), 0, GROUPS, dtype=jnp.int32)
    hot_offset = jax.random.randint(keys[1], (), 0, GROUP_EXPERTS, dtype=jnp.int32)
    row_noise = jax.random.randint(keys[2], (SOURCES, ROWS_DEV), 0, 4096, dtype=jnp.int32)
    row_score = row_noise * ROWS_DEV + jnp.arange(ROWS_DEV, dtype=jnp.int32)[None, :]
    hot_rows = lax.top_k(row_score, NODE_CAP)[1].astype(jnp.int32)
    row_ids = jnp.arange(ROWS_DEV, dtype=jnp.int32)
    has_hot = jnp.sum((hot_rows[:, None, :] == row_ids[None, :, None]).astype(jnp.int32), axis=-1, dtype=jnp.int32)
    group_noise = jax.random.randint(keys[3], (SOURCES, GROUPS), 0, 4096, dtype=jnp.int32)
    is_hot_group = (group_index == hot_group)[None, :]
    group_score = jnp.where(is_hot_group, 8192 * GROUPS, group_noise * GROUPS + group_index[None, :])
    order = lax.top_k(group_score, GROUPS)[1].astype(jnp.int32)
    others = order[:, 1:]
    other_count = TOPG - has_hot
    other_start = jnp.cumsum(other_count, axis=1, dtype=jnp.int32) - other_count
    slot_index = jnp.arange(TOPG, dtype=jnp.int32)[None, None, :]
    take_at = (other_start[:, :, None] + slot_index - has_hot[:, :, None] + (GROUPS - 1)) % (GROUPS - 1)
    others_wide = jnp.broadcast_to(others[:, None, :], (SOURCES, ROWS_DEV, GROUPS - 1))
    picked = jnp.take_along_axis(others_wide, take_at, axis=2)
    chosen_groups = jnp.where((has_hot[:, :, None] == 1) & (slot_index == 0), hot_group, picked).astype(jnp.int32)
    member = jnp.sum((chosen_groups[..., None] == group_index).astype(jnp.int32), axis=-2, dtype=jnp.int32)
    earlier = jnp.cumsum(member, axis=1, dtype=jnp.int32) - member
    is_hot = (group_index == hot_group)[None, None, :]
    offsets = jax.random.randint(keys[6], (SOURCES, 1, GROUPS), 0, GROUP_EXPERTS, dtype=jnp.int32)
    offsets = jnp.broadcast_to(jnp.where(is_hot, hot_offset, offsets), (SOURCES, ROWS_DEV, GROUPS))
    rank_in = jnp.take_along_axis(earlier, chosen_groups, axis=2)
    start_at = jnp.take_along_axis(offsets, chosen_groups, axis=2)
    pair_size = TOPK // TOPG
    within = (start_at[..., None] + pair_size * rank_in[..., None] + jnp.arange(pair_size, dtype=jnp.int32)) % GROUP_EXPERTS
    chosen = chosen_groups[..., None] * GROUP_EXPERTS + within
    return chosen.reshape(TOKENS, TOPK).astype(jnp.int32)


def steps_of(stream_key, extent, cuts, low, top_value):
    def one(dim, shards_of):
        steps = jax.random.uniform(jax.random.fold_in(jax.random.fold_in(stream_key, 6), dim), (shards_of,), jnp.float32, low / len(cuts), top_value / len(cuts))
        return jnp.repeat(jnp.exp(steps), extent[dim] // shards_of).reshape((-1,) + (1,) * (len(extent) - dim - 1))

    level = one(*cuts[0])
    for cut in cuts[1:]:
        level = level * one(*cut)
    return level


def centred(rng, extent, deviation, most, cuts=(), kind=jnp.bfloat16):
    factor_of = steps_of(rng, extent, cuts, -0.22, 0.18) if cuts else 1.0
    entries = jax.random.normal(rng, extent, jnp.float32) * deviation * factor_of
    return jnp.minimum(jnp.maximum(entries, -most), most).astype(kind)


def setup_inputs(seed: int = 0) -> dict:
    key_of = jax.random.split(jax.random.key(seed), 11)
    moe_in = centred(key_of[0], (TOKENS, D), 1.0, 6.0, ((0, 32),))
    route_ids = draw_route_ids(jax.random.fold_in(key_of[10], 71), 0)
    route_weights = jnp.clip(jnp.exp(math.log(0.6) - 2.4849067 * jax.random.uniform(key_of[2], (TOKENS, TOPK), jnp.float32) ** steps_of(key_of[2], (TOKENS, TOPK), ((0, 32),), -0.2, 0.2)), 0.05, 0.6)
    w_gate = centred(key_of[3], (EXPERTS, D, H), D ** -0.5, 0.09375, ((0, 32),))
    w_up = centred(key_of[4], (EXPERTS, D, H), D ** -0.5, 0.09375, ((0, 32),))
    w_down = centred(key_of[5], (EXPERTS, H, D), H ** -0.5, 0.1875, ((0, 32),))
    queries = draw_queries(jax.random.fold_in(key_of[10], 71), 0)
    cache_latent = draw_cache_latent(jax.random.fold_in(key_of[10], 71), 0)
    cache_rope = draw_cache_rope(jax.random.fold_in(key_of[10], 71), 0)
    lengths = draw_lengths(jax.random.fold_in(key_of[10], 71), 0)
    return dict(moe_in=moe_in, route_ids=route_ids, route_weights=route_weights, w_gate=w_gate, w_up=w_up, w_down=w_down, queries=queries, cache_latent=cache_latent, cache_rope=cache_rope, lengths=lengths)


score_scale = 192.0 ** -0.5
block_rows = 128


def expert_ffn(inputs, gate_one, up_one, down_one):
    gate_act = jnp.dot(inputs, gate_one, preferred_element_type=jnp.float32)
    up_act = jnp.dot(inputs, up_one, preferred_element_type=jnp.float32)
    hidden_act = (jax.nn.silu(gate_act) * up_act).astype(jnp.bfloat16)
    return jnp.dot(hidden_act, down_one, preferred_element_type=jnp.float32).astype(jnp.bfloat16)


def routed_experts(moe_in, route_ids, route_weights, w_gate, w_up, w_down):
    pair_count = TOKENS * TOPK
    pair_expert = route_ids.reshape(-1).astype(jnp.int32)
    pair_weight = route_weights.reshape(-1)
    ordering = jnp.argsort(pair_expert, stable=True).astype(jnp.int32)
    expert_index = jnp.arange(EXPERTS, dtype=jnp.int32)
    counts_all = jnp.sum((pair_expert[:, None] == expert_index[None, :]).astype(jnp.int32), axis=0, dtype=jnp.int32)
    starts_all = jnp.cumsum(counts_all, dtype=jnp.int32) - counts_all

    def expert_step(expert, total):
        count_here = counts_all[expert]
        start_here = starts_all[expert]
        gate_one = w_gate[expert]
        up_one = w_up[expert]
        down_one = w_down[expert]

        def block_step(block_index, accum):
            offsets = block_index * block_rows + jnp.arange(block_rows, dtype=jnp.int32)
            valid = offsets < count_here
            position = ordering[jnp.minimum(start_here + offsets, pair_count - 1)]
            source_row = position // TOPK
            result = expert_ffn(moe_in[source_row], gate_one, up_one, down_one)
            coeff = jnp.where(valid, pair_weight[position], 0.0)
            return accum.at[source_row].add(coeff[:, None] * result.astype(jnp.float32))

        blocks_here = (count_here + block_rows - 1) // block_rows
        return lax.fori_loop(0, blocks_here, block_step, total)

    total = lax.fori_loop(0, EXPERTS, expert_step, jnp.zeros((TOKENS, D), jnp.float32))
    return total.astype(jnp.bfloat16)


def attend_row(packed):
    query_row, latent_row, rope_row, length_row = packed
    scores = jnp.dot(query_row[:, :KV_RANK], latent_row.T, preferred_element_type=jnp.float32)
    scores = (scores + jnp.dot(query_row[:, KV_RANK:], rope_row, preferred_element_type=jnp.float32)) * score_scale
    positions = jnp.arange(CACHE, dtype=jnp.int32)
    scores = jnp.where(positions[None, :] < length_row, scores, -jnp.inf)
    peak = jnp.max(scores, axis=-1, keepdims=True)
    weights = jnp.exp(scores - peak)
    probs = (weights / jnp.sum(weights, axis=-1, keepdims=True)).astype(jnp.bfloat16)
    return jnp.dot(probs, latent_row, preferred_element_type=jnp.float32).astype(jnp.bfloat16)


def reference(moe_in, route_ids, route_weights, w_gate, w_up, w_down, queries, cache_latent, cache_rope, lengths):
    moe_out = routed_experts(moe_in, route_ids, route_weights, w_gate, w_up, w_down)
    attn_out = lax.map(attend_row, (queries, cache_latent, cache_rope, lengths))
    return (moe_out, attn_out)
```

```python
import functools

import jax
import jax.numpy as jnp
from jax import lax
from jax.experimental import pallas as pl
from jax.experimental.pallas import tpu as pltpu
from jax.sharding import PartitionSpec as P

score_scale = 192.0 ** (-0.5)
MESH = pl.DeviceIdType.MESH
ROUTE_LANES = 128
ATT_PIECES = 4


def expert_block(block, gate_one, up_one, down_one):
    model_width = block.shape[-1]
    rows_flat = block.reshape(-1, model_width)
    gate_act = jnp.dot(rows_flat, gate_one, preferred_element_type=jnp.float32)
    up_act = jnp.dot(rows_flat, up_one, preferred_element_type=jnp.float32)
    hidden_act = (jax.nn.silu(gate_act) * up_act).astype(jnp.bfloat16)
    result = jnp.dot(hidden_act, down_one, preferred_element_type=jnp.float32).astype(jnp.bfloat16)
    return result.reshape(block.shape)


def attention(queries, cache_latent, cache_rope, lengths):
    kv_width = cache_latent.shape[-1]
    scores = jnp.einsum(
        "rhc,rkc->rhk", queries[:, :, :kv_width], cache_latent, preferred_element_type=jnp.float32
    )
    scores = (
        scores
        + jnp.einsum(
            "rhc,rck->rhk", queries[:, :, kv_width:], cache_rope, preferred_element_type=jnp.float32
        )
    ) * score_scale
    positions = jnp.arange(cache_latent.shape[1], dtype=jnp.int32)
    scores = jnp.where(positions[None, None, :] < lengths[:, None, None], scores, -jnp.inf)
    peak = jnp.max(scores, axis=-1, keepdims=True)
    weights = jnp.exp(scores - peak)
    probs = (weights / jnp.sum(weights, axis=-1, keepdims=True)).astype(jnp.bfloat16)
    return jnp.einsum(
        "rhk,rkc->rhc", probs, cache_latent, preferred_element_type=jnp.float32
    ).astype(jnp.bfloat16)


def local_general(
    moe_in,
    route_ids,
    route_weights,
    w_gate,
    w_up,
    w_down,
    queries,
    cache_latent,
    cache_rope,
    lengths,
):
    attn_out = attention(queries, cache_latent, cache_rope, lengths)
    expert_count = lax.axis_size("node") * lax.axis_size("local")
    row_count, model_width = moe_in.shape
    top_count = route_ids.shape[1]
    capacity = 2 * row_count * top_count // expert_count
    row_index = jnp.broadcast_to(jnp.arange(row_count, dtype=jnp.int32)[:, None], route_ids.shape)
    padded = jnp.concatenate([moe_in, jnp.zeros((1, model_width), moe_in.dtype)], axis=0)
    expert_hits = (
        route_ids[:, :, None] == jnp.arange(expert_count, dtype=jnp.int32)[None, None, :]
    ).astype(jnp.int32)
    present = jnp.sum(expert_hits, axis=1, dtype=jnp.int32)
    earlier = jnp.cumsum(present, axis=0, dtype=jnp.int32) - present
    rank_of = jnp.sum(expert_hits * earlier[:, None, :], axis=-1, dtype=jnp.int32)
    slot_of = route_ids * capacity + rank_of
    table = (
        jnp.full((expert_count * capacity,), row_count, jnp.int32)
        .at[slot_of.reshape(-1)]
        .set(row_index.reshape(-1))
    )
    outgoing = padded[table].reshape(expert_count, capacity, model_width)
    result = expert_block(
        lax.all_to_all(outgoing, ("node", "local"), split_axis=0, concat_axis=0, tiled=True),
        w_gate[0],
        w_up[0],
        w_down[0],
    )
    returned = lax.all_to_all(result, ("node", "local"), split_axis=0, concat_axis=0, tiled=True)
    picked = returned.reshape(expert_count * capacity, model_width)[slot_of]
    total = jnp.einsum("rk,rkd->rd", route_weights, picked.astype(jnp.float32))
    return (total.astype(jnp.bfloat16), attn_out)


def fused_kernel(
    dims,
    capacity,
    x_ref,
    ids_ref,
    rw_ref,
    len_ref,
    q_ref,
    gate_hbm,
    up_hbm,
    down_hbm,
    latent_hbm,
    rope_hbm,
    moe_ref,
    attn_ref,
    gathered,
    part,
    recv_core,
    sum_core,
    recv_one,
    sum_one,
    recv_two,
    sum_two,
    recv_z,
    gate_w,
    up_w,
    down_w,
    latent,
    rope,
    scores,
    attn_acc,
    gate_acc,
    up_acc,
    pick,
    spread,
    load_sem,
    cache_sem,
    ag_send,
    ag_recv,
    rs_send,
    rs_recv,
):
    ny, nx, nc, nz = dims
    rows, width = x_ref.shape
    chunks = len(gathered)
    cw = width // chunks
    tokens = ny * nx * nc * nz * rows
    slots_total = ny * nx * nc * nz * capacity
    hidden = gate_w.shape[1]
    f32, bf16 = jnp.float32, jnp.bfloat16

    node = lax.axis_index("node")
    z = lax.axis_index("local")
    core = lax.rem(node, nc)
    x = lax.rem(node // nc, nx)
    y = node // (nc * nx)
    me = node * nz + z

    def device(yy, xx, cc, zz):
        return ((yy * nx + xx) * nc + cc, zz)

    core_dev = device(y, x, 1 - core, z)
    x_dev = device(y, 1 - x, core, z)
    y_dev = device(1 - y, x, core, z)
    z_at = [lax.rem(z + o, nz) for o in range(nz)]
    z_devs = [device(y, x, core, z_at[o]) for o in range(1, nz)]

    barrier = pltpu.get_barrier_semaphore()
    for dev in [core_dev, x_dev, y_dev] + z_devs:
        pl.semaphore_signal(barrier, inc=1, device_id=dev, device_id_type=MESH)

    cache_loads = [
        pltpu.make_async_copy(latent_hbm.at[0], latent, cache_sem.at[0]),
        pltpu.make_async_copy(rope_hbm.at[0], rope, cache_sem.at[1]),
    ]
    for load in cache_loads:
        load.start()
    gate_loads, up_loads, down_loads = [], [], []
    for c in range(chunks):
        at = pl.ds(c * cw, cw)
        gate_loads.append(
            pltpu.make_async_copy(gate_hbm.at[0, at], gate_w.at[at], load_sem.at[0, c])
        )
        up_loads.append(pltpu.make_async_copy(up_hbm.at[0, at], up_w.at[at], load_sem.at[1, c]))
        down_loads.append(
            pltpu.make_async_copy(down_hbm.at[0, :, at], down_w.at[c], load_sem.at[2, c])
        )
    for c in range(chunks):
        gate_loads[c].start()
        up_loads[c].start()
    for c in range(chunks):
        down_loads[c].start()

    lanes = lax.broadcasted_iota(jnp.int32, (rows, ROUTE_LANES), 1)
    ids = jnp.transpose(ids_ref[...])
    rw = jnp.transpose(rw_ref[...])
    table = jnp.zeros((rows, ROUTE_LANES), f32)
    for k in range(ids.shape[1]):
        table = table + jnp.where(lanes == ids[:, k : k + 1], rw[:, k : k + 1], 0.0)
    gathered[0][y, x, core, z, :, :ROUTE_LANES] = table.astype(bf16)
    gathered[0][y, x, core, z, :, ROUTE_LANES:] = x_ref[:, :cw]
    for c in range(1, chunks):
        gathered[c][y, x, core, z] = x_ref[:, c * cw : (c + 1) * cw]

    pl.semaphore_wait(barrier, 2 + nz)

    sends = []

    def push(src, dst, send_sem, recv_sem, dev):
        copy = pltpu.make_async_remote_copy(
            src_ref=src,
            dst_ref=dst,
            send_sem=send_sem,
            recv_sem=recv_sem,
            device_id=dev,
            device_id_type=MESH,
        )
        copy.start()
        sends.append(copy)

    def arrived(dst, send_sem, recv_sem, dev):
        pltpu.make_async_remote_copy(
            src_ref=dst,
            dst_ref=dst,
            send_sem=send_sem,
            recv_sem=recv_sem,
            device_id=dev,
            device_id_type=MESH,
        ).wait_recv()

    def gather_z(c):
        own = gathered[c].at[y, x, core, z]
        for o in range(1, nz):
            push(own, own, ag_send.at[c, o - 1], ag_recv.at[c, o - 1], z_devs[o - 1])

    def gather_z_wait(c):
        for o in range(1, nz):
            arrived(
                gathered[c].at[y, x, core, z_at[nz - o]],
                ag_send.at[c, o - 1],
                ag_recv.at[c, o - 1],
                z_devs[nz - o - 1],
            )

    def gather_views(c):
        first = gathered[c].at[y, x, core]
        if c % 2 == 0:
            return [
                (first, gathered[c].at[y, 1 - x, core], x_dev),
                (gathered[c].at[y, :, core], gathered[c].at[1 - y, :, core], y_dev),
                (gathered[c].at[:, :, core], gathered[c].at[:, :, 1 - core], core_dev),
            ]
        return [
            (first, gathered[c].at[1 - y, x, core], y_dev),
            (gathered[c].at[:, x, core], gathered[c].at[:, 1 - x, core], x_dev),
            (gathered[c].at[:, :, core], gathered[c].at[:, :, 1 - core], core_dev),
        ]

    def gather_push(c, phase):
        src, _, dev = gather_views(c)[phase]
        k = nz - 1 + phase
        push(src, src, ag_send.at[c, k], ag_recv.at[c, k], dev)

    def gather_wait(c, phase):
        _, dst, dev = gather_views(c)[phase]
        k = nz - 1 + phase
        arrived(dst, ag_send.at[c, k], ag_recv.at[c, k], dev)

    kv = latent.shape[1]
    cache = latent.shape[0]
    piece = cache // ATT_PIECES
    length = len_ref[0]

    def score_piece(i):
        at = slice(i * piece, (i + 1) * piece)
        s = jnp.dot(latent[at, :], q_ref[0, :kv, :], preferred_element_type=f32)
        s = s + lax.dot_general(
            rope[:, at], q_ref[0, kv:, :], (((0,), (0,)), ((), ())), preferred_element_type=f32
        )
        positions = lax.broadcasted_iota(jnp.int32, s.shape, 0) + i * piece
        scores[at, :] = jnp.where(positions < length, s * score_scale, -jnp.inf)

    def soft():
        s = scores[...]
        e = jnp.exp(s - jnp.max(s, axis=0, keepdims=True))
        scores[...] = e / jnp.sum(e, axis=0, keepdims=True)

    def value_piece(i):
        at = slice(i * piece, (i + 1) * piece)
        got = lax.dot_general(
            scores[at, :].astype(bf16),
            latent[at, :],
            (((0,), (0,)), ((), ())),
            preferred_element_type=f32,
        )
        if i == 0:
            attn_acc[...] = got
        elif i < ATT_PIECES - 1:
            attn_acc[...] += got
        else:
            attn_ref[0] = (attn_acc[...] + got).astype(bf16)

    def first_piece():
        for load in cache_loads:
            load.wait()
        score_piece(0)

    tasks = [first_piece]
    tasks += [functools.partial(score_piece, i) for i in range(1, ATT_PIECES)]
    tasks += [soft]
    tasks += [functools.partial(value_piece, i) for i in range(ATT_PIECES)]

    def route():
        sent = gathered[0][:, :, :, :, :, :ROUTE_LANES].reshape(tokens, ROUTE_LANES)
        mine = (lax.broadcasted_iota(jnp.int32, (16, ROUTE_LANES), 1) == me).astype(bf16)
        weight = lax.dot_general(
            mine, sent, (((1,), (1,)), ((), ())), preferred_element_type=f32
        )
        present = weight > 0.0
        t_from = lax.broadcasted_iota(jnp.int32, (tokens, tokens), 0)
        t_to = lax.broadcasted_iota(jnp.int32, (tokens, tokens), 1)
        before = ((t_from < t_to) & (t_from // rows == t_to // rows)).astype(bf16)
        rank = jnp.dot(present.astype(bf16), before, preferred_element_type=f32)
        base = (lax.broadcasted_iota(jnp.int32, (16, tokens), 1) // rows) * capacity
        slot = jnp.where(present, rank + base.astype(f32), -1.0)
        slot_id = lax.broadcasted_iota(jnp.int32, (slots_total, tokens), 0).astype(f32)
        hit = slot[0:1, :] == slot_id
        pick[...] = hit.astype(bf16)
        spread[...] = jnp.transpose(jnp.where(hit, weight[0:1, :], 0.0)).astype(bf16)

    def expert_in(c):
        g = gathered[c][...] if c else gathered[c][:, :, :, :, :, ROUTE_LANES:]
        rows_in = jnp.dot(
            pick[...], g.reshape(tokens, cw), preferred_element_type=f32
        ).astype(bf16)
        gate_loads[c].wait()
        up_loads[c].wait()
        at = slice(c * cw, (c + 1) * cw)
        for acc, w in ((gate_acc, gate_w), (up_acc, up_w)):
            got = jnp.dot(rows_in, w[at, :], preferred_element_type=f32)
            if c == 0:
                acc[...] = got
            else:
                acc[...] += got

    for c in range(chunks):
        gather_z(c)
    for s in range(chunks + 3):
        if s < chunks:
            gather_z_wait(s)
            gather_push(s, 0)
        for phase in range(2):
            c = s - 1 - phase
            if 0 <= c < chunks:
                gather_wait(c, phase)
                gather_push(c, phase + 1)
        if tasks:
            tasks.pop(0)()
        c = s - 3
        if 0 <= c < chunks:
            gather_wait(c, 2)
            if c == 0:
                route()
            expert_in(c)
    for task in tasks:
        task()

    gate = gate_acc[...]
    hidden_act = (gate / (1.0 + jnp.exp(-gate)) * up_acc[...]).astype(bf16)

    def add_to(dst, a, b):
        dst[...] = (a.astype(f32) + b.astype(f32)).astype(bf16)

    def out_views(c):
        if c % 2 == 0:
            return [
                (part[c].at[:, :, 1 - core], recv_core[c], core_dev),
                (sum_core[c].at[1 - y], recv_one[c], y_dev),
                (sum_one[c].at[1 - x], recv_two[c], x_dev),
            ]
        return [
            (part[c].at[:, :, 1 - core], recv_core[c], core_dev),
            (sum_core[c].at[:, 1 - x], recv_one[c], x_dev),
            (sum_one[c].at[1 - y], recv_two[c], y_dev),
        ]

    def out_push(c, phase):
        src, dst, dev = out_views(c)[phase]
        push(src, dst, rs_send.at[c, phase], rs_recv.at[c, phase], dev)

    def out_wait(c, phase):
        _, dst, dev = out_views(c)[phase]
        arrived(dst, rs_send.at[c, phase], rs_recv.at[c, phase], dev)

    def stage_zero(c):
        down_loads[c].wait()
        out = jnp.dot(hidden_act, down_w[c], preferred_element_type=f32).astype(bf16)
        got = jnp.dot(spread[...], out, preferred_element_type=f32).astype(bf16)
        part[c][...] = got.reshape(part[c].shape)
        out_push(c, 0)

    def stage_one(c):
        out_wait(c, 0)
        add_to(sum_core[c], part[c][:, :, core], recv_core[c][...])
        out_push(c, 1)

    def stage_two(c):
        out_wait(c, 1)
        kept = sum_core[c][y] if c % 2 == 0 else sum_core[c][:, x]
        add_to(sum_one[c], kept, recv_one[c][...])
        out_push(c, 2)

    def stage_three(c):
        out_wait(c, 2)
        kept = sum_one[c][x] if c % 2 == 0 else sum_one[c][y]
        add_to(sum_two[c], kept, recv_two[c][...])
        for o in range(1, nz):
            push(
                sum_two[c].at[z_at[o]],
                recv_z[c].at[o - 1],
                rs_send.at[c, 2 + o],
                rs_recv.at[c, 2 + o],
                z_devs[o - 1],
            )

    def stage_four(c):
        total = sum_two[c][z].astype(f32)
        for o in range(1, nz):
            arrived(
                recv_z[c].at[o - 1], rs_send.at[c, 2 + o], rs_recv.at[c, 2 + o], z_devs[nz - o - 1]
            )
            total = total + recv_z[c][o - 1].astype(f32)
        moe_ref[:, c * cw : (c + 1) * cw] = total.astype(bf16)

    stages = [stage_zero, stage_one, stage_two, stage_three, stage_four]
    for s in range(chunks + len(stages) - 1):
        for k, stage in enumerate(stages):
            c = s - k
            if 0 <= c < chunks:
                stage(c)

    for copy in sends:
        copy.wait_send()


def local_fused(
    dims,
    moe_in,
    route_ids,
    route_weights,
    w_gate,
    w_up,
    w_down,
    queries,
    cache_latent,
    cache_rope,
    lengths,
):
    ny, nx, nc, nz = dims
    experts = ny * nx * nc * nz
    rows, width = moe_in.shape
    capacity = 2 * rows * route_ids.shape[1] // experts
    hidden = w_gate.shape[2]
    cache, kv = cache_latent.shape[1:]
    heads = queries.shape[1]
    tokens = experts * rows
    chunks = 7
    cw = width // chunks
    bf16, f32 = jnp.bfloat16, jnp.float32

    def each(shape, extra=0):
        return [
            pltpu.VMEM(shape + (cw + (extra if c == 0 else 0),), bf16) for c in range(chunks)
        ]

    vmem = pl.BlockSpec(memory_space=pltpu.VMEM)
    hbm = pl.BlockSpec(memory_space=pl.ANY)
    moe_out, attn_out = pl.pallas_call(
        functools.partial(fused_kernel, dims, capacity),
        out_shape=(
            jax.ShapeDtypeStruct((rows, width), bf16),
            jax.ShapeDtypeStruct((1, heads, kv), bf16),
        ),
        in_specs=[
            vmem,
            vmem,
            vmem,
            pl.BlockSpec(memory_space=pltpu.SMEM),
            vmem,
            hbm,
            hbm,
            hbm,
            hbm,
            hbm,
        ],
        out_specs=(vmem, vmem),
        scratch_shapes=[
            each((ny, nx, nc, nz, rows), ROUTE_LANES),
            each((ny, nx, nc, nz, rows)),
            each((ny, nx, nz, rows)),
            each((ny, nx, nz, rows)),
            each((2, nz, rows)),
            each((2, nz, rows)),
            each((nz, rows)),
            each((nz, rows)),
            each((nz - 1, rows)),
            pltpu.VMEM((width, hidden), bf16),
            pltpu.VMEM((width, hidden), bf16),
            pltpu.VMEM((chunks, hidden, cw), bf16),
            pltpu.VMEM((cache, kv), bf16),
            pltpu.VMEM(cache_rope.shape[1:], bf16),
            pltpu.VMEM((cache, heads), f32),
            pltpu.VMEM((heads, kv), f32),
            pltpu.VMEM((experts * capacity, hidden), f32),
            pltpu.VMEM((experts * capacity, hidden), f32),
            pltpu.VMEM((experts * capacity, tokens), bf16),
            pltpu.VMEM((tokens, experts * capacity), bf16),
            pltpu.SemaphoreType.DMA((3, chunks)),
            pltpu.SemaphoreType.DMA((2,)),
            pltpu.SemaphoreType.DMA((chunks, nz + 2)),
            pltpu.SemaphoreType.DMA((chunks, nz + 2)),
            pltpu.SemaphoreType.DMA((chunks, nz + 2)),
            pltpu.SemaphoreType.DMA((chunks, nz + 2)),
        ],
        compiler_params=pltpu.CompilerParams(
            collective_id=0, has_side_effects=True, vmem_limit_bytes=60 * 1024 * 1024
        ),
        name="fused_moe_attention",
    )(
        moe_in,
        jnp.transpose(route_ids),
        jnp.transpose(route_weights),
        lengths,
        jnp.transpose(queries, (0, 2, 1)),
        w_gate,
        w_up,
        w_down,
        cache_latent,
        cache_rope,
    )
    return moe_out, attn_out


def solution(mesh):
    placed = (
        P(("node", "local"), None),
        P(("node", "local"), None),
        P(("node", "local"), None),
        P(("node", "local"), None, None),
        P(("node", "local"), None, None),
        P(("node", "local"), None, None),
        P(("node", "local"), None, None),
        P(("node", "local"), None, None),
        P(("node", "local"), None, None),
        P(("node", "local")),
    )
    if mesh.shape["node"] == 8 and mesh.shape["local"] == 4:
        local = functools.partial(local_fused, (2, 2, 2, 4))
    else:
        local = local_general
    return jax.shard_map(
        local,
        mesh=mesh,
        in_specs=placed,
        out_specs=(P(("node", "local"), None), P(("node", "local"), None, None)),
        check_vma=False,
    )
```

```python
import functools

import jax
import jax.numpy as jnp
from jax import lax
from jax.experimental import pallas as pl
from jax.experimental.pallas import tpu as pltpu
from jax.sharding import PartitionSpec as P

score_scale = 192.0 ** (-0.5)
MESH = pl.DeviceIdType.MESH
ROUTE_LANES = 128
ATT_PIECES = 4
IN_STEPS = 7
OUT_LAGS = (0, 1, 3, 5, 7)
CHUNKS = 7
VMEM_BYTES = 60 * 1024 * 1024


def expert_block(block, gate_one, up_one, down_one):
    model_width = block.shape[-1]
    rows_flat = block.reshape(-1, model_width)
    gate_act = jnp.dot(rows_flat, gate_one, preferred_element_type=jnp.float32)
    up_act = jnp.dot(rows_flat, up_one, preferred_element_type=jnp.float32)
    hidden_act = (jax.nn.silu(gate_act) * up_act).astype(jnp.bfloat16)
    result = jnp.dot(hidden_act, down_one, preferred_element_type=jnp.float32).astype(jnp.bfloat16)
    return result.reshape(block.shape)


def attention(queries, cache_latent, cache_rope, lengths):
    kv_width = cache_latent.shape[-1]
    scores = jnp.einsum(
        "rhc,rkc->rhk", queries[:, :, :kv_width], cache_latent, preferred_element_type=jnp.float32
    )
    scores = (
        scores
        + jnp.einsum(
            "rhc,rck->rhk", queries[:, :, kv_width:], cache_rope, preferred_element_type=jnp.float32
        )
    ) * score_scale
    positions = jnp.arange(cache_latent.shape[1], dtype=jnp.int32)
    scores = jnp.where(positions[None, None, :] < lengths[:, None, None], scores, -jnp.inf)
    peak = jnp.max(scores, axis=-1, keepdims=True)
    weights = jnp.exp(scores - peak)
    probs = (weights / jnp.sum(weights, axis=-1, keepdims=True)).astype(jnp.bfloat16)
    return jnp.einsum(
        "rhk,rkc->rhc", probs, cache_latent, preferred_element_type=jnp.float32
    ).astype(jnp.bfloat16)


def local_general(
    moe_in,
    route_ids,
    route_weights,
    w_gate,
    w_up,
    w_down,
    queries,
    cache_latent,
    cache_rope,
    lengths,
):
    attn_out = attention(queries, cache_latent, cache_rope, lengths)
    expert_count = lax.axis_size("node") * lax.axis_size("local")
    row_count, model_width = moe_in.shape
    top_count = route_ids.shape[1]
    capacity = 2 * row_count * top_count // expert_count
    row_index = jnp.broadcast_to(jnp.arange(row_count, dtype=jnp.int32)[:, None], route_ids.shape)
    padded = jnp.concatenate([moe_in, jnp.zeros((1, model_width), moe_in.dtype)], axis=0)
    expert_hits = (
        route_ids[:, :, None] == jnp.arange(expert_count, dtype=jnp.int32)[None, None, :]
    ).astype(jnp.int32)
    present = jnp.sum(expert_hits, axis=1, dtype=jnp.int32)
    earlier = jnp.cumsum(present, axis=0, dtype=jnp.int32) - present
    rank_of = jnp.sum(expert_hits * earlier[:, None, :], axis=-1, dtype=jnp.int32)
    slot_of = route_ids * capacity + rank_of
    table = (
        jnp.full((expert_count * capacity,), row_count, jnp.int32)
        .at[slot_of.reshape(-1)]
        .set(row_index.reshape(-1))
    )
    outgoing = padded[table].reshape(expert_count, capacity, model_width)
    result = expert_block(
        lax.all_to_all(outgoing, ("node", "local"), split_axis=0, concat_axis=0, tiled=True),
        w_gate[0],
        w_up[0],
        w_down[0],
    )
    returned = lax.all_to_all(result, ("node", "local"), split_axis=0, concat_axis=0, tiled=True)
    picked = returned.reshape(expert_count * capacity, model_width)[slot_of]
    total = jnp.einsum("rk,rkd->rd", route_weights, picked.astype(jnp.float32))
    return (total.astype(jnp.bfloat16), attn_out)


def fused_kernel(
    dims,
    capacity,
    x_ref,
    ids_ref,
    rw_ref,
    len_ref,
    q_ref,
    gate_hbm,
    up_hbm,
    down_hbm,
    latent_hbm,
    rope_hbm,
    moe_ref,
    attn_ref,
    gathered,
    part,
    recv_core,
    sum_core,
    recv_one,
    sum_one,
    recv_two,
    sum_two,
    recv_z,
    gate_w,
    up_w,
    down_w,
    latent,
    rope,
    scores,
    attn_acc,
    gate_acc,
    up_acc,
    pick,
    spread,
    load_sem,
    cache_sem,
    ag_send,
    ag_recv,
    rs_send,
    rs_recv,
):
    ny, nx, nc, nz = dims
    rows, width = x_ref.shape
    chunks = len(gathered)
    cw = width // chunks
    merge = chunks // IN_STEPS
    tokens = ny * nx * nc * nz * rows
    slots_total = ny * nx * nc * nz * capacity
    hidden = gate_w.shape[1]
    f32, bf16 = jnp.float32, jnp.bfloat16

    node = lax.axis_index("node")
    z = lax.axis_index("local")
    core = lax.rem(node, nc)
    x = lax.rem(node // nc, nx)
    y = node // (nc * nx)
    me = node * nz + z

    def device(yy, xx, cc, zz):
        return ((yy * nx + xx) * nc + cc, zz)

    core_dev = device(y, x, 1 - core, z)
    x_dev = device(y, 1 - x, core, z)
    y_dev = device(1 - y, x, core, z)
    z_at = [lax.rem(z + o, nz) for o in range(nz)]
    z_devs = [device(y, x, core, z_at[o]) for o in range(1, nz)]

    barrier = pltpu.get_barrier_semaphore()
    for dev in [core_dev, x_dev, y_dev] + z_devs:
        pl.semaphore_signal(barrier, inc=1, device_id=dev, device_id_type=MESH)

    cache_loads = [
        pltpu.make_async_copy(latent_hbm.at[0], latent, cache_sem.at[0]),
        pltpu.make_async_copy(rope_hbm.at[0], rope, cache_sem.at[1]),
    ]
    for load in cache_loads:
        load.start()
    gate_loads, up_loads, down_loads = [], [], []
    for m in range(chunks // merge):
        at = pl.ds(m * merge * cw, merge * cw)
        gate_loads.append(
            pltpu.make_async_copy(gate_hbm.at[0, at], gate_w.at[at], load_sem.at[0, m])
        )
        up_loads.append(pltpu.make_async_copy(up_hbm.at[0, at], up_w.at[at], load_sem.at[1, m]))
    for c in range(chunks):
        at = pl.ds(c * cw, cw)
        down_loads.append(
            pltpu.make_async_copy(down_hbm.at[0, :, at], down_w.at[c], load_sem.at[2, c])
        )
    for m in range(chunks // merge):
        gate_loads[m].start()
        up_loads[m].start()
    for c in range(chunks):
        down_loads[c].start()

    lanes = lax.broadcasted_iota(jnp.int32, (rows, ROUTE_LANES), 1)
    ids = jnp.transpose(ids_ref[...])
    rw = jnp.transpose(rw_ref[...])
    table = jnp.zeros((rows, ROUTE_LANES), f32)
    for k in range(ids.shape[1]):
        table = table + jnp.where(lanes == ids[:, k : k + 1], rw[:, k : k + 1], 0.0)
    gathered[0][y, x, core, z, :, :ROUTE_LANES] = table.astype(bf16)
    gathered[0][y, x, core, z, :, ROUTE_LANES:] = x_ref[:, :cw]
    for c in range(1, chunks):
        gathered[c][y, x, core, z] = x_ref[:, c * cw : (c + 1) * cw]

    pl.semaphore_wait(barrier, 2 + nz)

    sends = []

    def push(src, dst, send_sem, recv_sem, dev):
        copy = pltpu.make_async_remote_copy(
            src_ref=src,
            dst_ref=dst,
            send_sem=send_sem,
            recv_sem=recv_sem,
            device_id=dev,
            device_id_type=MESH,
        )
        copy.start()
        sends.append(copy)

    def arrived(dst, send_sem, recv_sem, dev):
        pltpu.make_async_remote_copy(
            src_ref=dst,
            dst_ref=dst,
            send_sem=send_sem,
            recv_sem=recv_sem,
            device_id=dev,
            device_id_type=MESH,
        ).wait_recv()

    def gather_z(c):
        own = gathered[c].at[y, x, core, z]
        for o in range(1, nz):
            push(own, own, ag_send.at[c, o - 1], ag_recv.at[c, o - 1], z_devs[o - 1])

    def gather_z_wait(c):
        for o in range(1, nz):
            arrived(
                gathered[c].at[y, x, core, z_at[nz - o]],
                ag_send.at[c, o - 1],
                ag_recv.at[c, o - 1],
                z_devs[nz - o - 1],
            )

    def gather_views(c):
        first = gathered[c].at[y, x, core]
        if c % 2 == 0:
            return [
                (first, gathered[c].at[y, 1 - x, core], x_dev),
                (gathered[c].at[y, :, core], gathered[c].at[1 - y, :, core], y_dev),
                (gathered[c].at[:, :, core], gathered[c].at[:, :, 1 - core], core_dev),
            ]
        return [
            (first, gathered[c].at[1 - y, x, core], y_dev),
            (gathered[c].at[:, x, core], gathered[c].at[:, 1 - x, core], x_dev),
            (gathered[c].at[:, :, core], gathered[c].at[:, :, 1 - core], core_dev),
        ]

    def gather_push(c, phase):
        src, _, dev = gather_views(c)[phase]
        k = nz - 1 + phase
        push(src, src, ag_send.at[c, k], ag_recv.at[c, k], dev)

    def gather_wait(c, phase):
        _, dst, dev = gather_views(c)[phase]
        k = nz - 1 + phase
        arrived(dst, ag_send.at[c, k], ag_recv.at[c, k], dev)

    kv = latent.shape[1]
    cache = latent.shape[0]
    piece = cache // ATT_PIECES
    length = len_ref[0]

    def score_piece(i):
        at = slice(i * piece, (i + 1) * piece)
        s = jnp.dot(latent[at, :], q_ref[0, :kv, :], preferred_element_type=f32)
        s = s + lax.dot_general(
            rope[:, at], q_ref[0, kv:, :], (((0,), (0,)), ((), ())), preferred_element_type=f32
        )
        positions = lax.broadcasted_iota(jnp.int32, s.shape, 0) + i * piece
        scores[at, :] = jnp.where(positions < length, s * score_scale, -jnp.inf)

    def soft():
        s = scores[...]
        e = jnp.exp(s - jnp.max(s, axis=0, keepdims=True))
        scores[...] = e / jnp.sum(e, axis=0, keepdims=True)

    def value_piece(i):
        at = slice(i * piece, (i + 1) * piece)
        got = lax.dot_general(
            scores[at, :].astype(bf16),
            latent[at, :],
            (((0,), (0,)), ((), ())),
            preferred_element_type=f32,
        )
        if i == 0:
            attn_acc[...] = got
        elif i < ATT_PIECES - 1:
            attn_acc[...] += got
        else:
            attn_ref[0] = (attn_acc[...] + got).astype(bf16)

    def first_piece():
        for load in cache_loads:
            load.wait()
        score_piece(0)

    tasks = [first_piece]
    tasks += [functools.partial(score_piece, i) for i in range(1, ATT_PIECES)]
    tasks += [soft]
    tasks += [functools.partial(value_piece, i) for i in range(ATT_PIECES)]

    def route():
        sent = gathered[0][:, :, :, :, :, :ROUTE_LANES].reshape(tokens, ROUTE_LANES)
        mine = (lax.broadcasted_iota(jnp.int32, (16, ROUTE_LANES), 1) == me).astype(bf16)
        weight = lax.dot_general(
            mine, sent, (((1,), (1,)), ((), ())), preferred_element_type=f32
        )
        present = weight > 0.0
        t_from = lax.broadcasted_iota(jnp.int32, (tokens, tokens), 0)
        t_to = lax.broadcasted_iota(jnp.int32, (tokens, tokens), 1)
        before = ((t_from < t_to) & (t_from // rows == t_to // rows)).astype(bf16)
        rank = jnp.dot(present.astype(bf16), before, preferred_element_type=f32)
        base = (lax.broadcasted_iota(jnp.int32, (16, tokens), 1) // rows) * capacity
        slot = jnp.where(present, rank + base.astype(f32), -1.0)
        slot_id = lax.broadcasted_iota(jnp.int32, (slots_total, tokens), 0).astype(f32)
        hit = slot[0:1, :] == slot_id
        pick[...] = hit.astype(bf16)
        spread[...] = jnp.transpose(jnp.where(hit, weight[0:1, :], 0.0)).astype(bf16)

    def expert_in(m):
        picked = []
        for c in range(m * merge, (m + 1) * merge):
            g = gathered[c][...] if c else gathered[c][:, :, :, :, :, ROUTE_LANES:]
            picked.append(
                jnp.dot(pick[...], g.reshape(tokens, cw), preferred_element_type=f32).astype(bf16)
            )
        rows_in = picked[0] if merge == 1 else jnp.concatenate(picked, axis=1)
        gate_loads[m].wait()
        up_loads[m].wait()
        at = slice(m * merge * cw, (m + 1) * merge * cw)
        for acc, w in ((gate_acc, gate_w), (up_acc, up_w)):
            got = jnp.dot(rows_in, w[at, :], preferred_element_type=f32)
            if m == 0:
                acc[...] = got
            else:
                acc[...] += got

    for c in range(chunks):
        gather_z(c)
    for s in range(chunks + 5):
        if s < chunks:
            gather_z_wait(s)
            gather_push(s, 0)
        for phase in range(2):
            c = s - 2 - 2 * phase
            if 0 <= c < chunks:
                gather_wait(c, phase)
                gather_push(c, phase + 1)
        for _ in range(2 if s < 4 else 1):
            if tasks:
                tasks.pop(0)()
        c = s - 5
        if 0 <= c < chunks:
            gather_wait(c, 2)
            if c == 0:
                route()
            if c % merge == merge - 1:
                expert_in(c // merge)
    for task in tasks:
        task()

    gate = gate_acc[...]
    hidden_act = (gate / (1.0 + jnp.exp(-gate)) * up_acc[...]).astype(bf16)

    def add_to(dst, a, b):
        dst[...] = (a.astype(f32) + b.astype(f32)).astype(bf16)

    def out_views(c):
        if c % 2 == 0:
            return [
                (part[c].at[:, :, 1 - core], recv_core[c], core_dev),
                (sum_core[c].at[1 - y], recv_one[c], y_dev),
                (sum_one[c].at[1 - x], recv_two[c], x_dev),
            ]
        return [
            (part[c].at[:, :, 1 - core], recv_core[c], core_dev),
            (sum_core[c].at[:, 1 - x], recv_one[c], x_dev),
            (sum_one[c].at[1 - y], recv_two[c], y_dev),
        ]

    def out_push(c, phase):
        src, dst, dev = out_views(c)[phase]
        push(src, dst, rs_send.at[c, phase], rs_recv.at[c, phase], dev)

    def out_wait(c, phase):
        _, dst, dev = out_views(c)[phase]
        arrived(dst, rs_send.at[c, phase], rs_recv.at[c, phase], dev)

    def stage_zero(c):
        down_loads[c].wait()
        out = jnp.dot(hidden_act, down_w[c], preferred_element_type=f32).astype(bf16)
        got = jnp.dot(spread[...], out, preferred_element_type=f32).astype(bf16)
        part[c][...] = got.reshape(part[c].shape)
        out_push(c, 0)

    def stage_one(c):
        out_wait(c, 0)
        add_to(sum_core[c], part[c][:, :, core], recv_core[c][...])
        out_push(c, 1)

    def stage_two(c):
        out_wait(c, 1)
        kept = sum_core[c][y] if c % 2 == 0 else sum_core[c][:, x]
        add_to(sum_one[c], kept, recv_one[c][...])
        out_push(c, 2)

    def stage_three(c):
        out_wait(c, 2)
        kept = sum_one[c][x] if c % 2 == 0 else sum_one[c][y]
        add_to(sum_two[c], kept, recv_two[c][...])
        for o in range(1, nz):
            push(
                sum_two[c].at[z_at[o]],
                recv_z[c].at[o - 1],
                rs_send.at[c, 2 + o],
                rs_recv.at[c, 2 + o],
                z_devs[o - 1],
            )

    def stage_four(c):
        total = sum_two[c][z].astype(f32)
        for o in range(1, nz):
            arrived(
                recv_z[c].at[o - 1], rs_send.at[c, 2 + o], rs_recv.at[c, 2 + o], z_devs[nz - o - 1]
            )
            total = total + recv_z[c][o - 1].astype(f32)
        moe_ref[:, c * cw : (c + 1) * cw] = total.astype(bf16)

    stages = [stage_zero, stage_one, stage_two, stage_three, stage_four]
    for s in range(chunks + OUT_LAGS[-1]):
        for lag, stage in zip(OUT_LAGS, stages):
            c = s - lag
            if 0 <= c < chunks:
                stage(c)

    for copy in sends:
        copy.wait_send()


def hand_on(moe_from, attn_from, moe_to, attn_to, sem):
    copies = [
        pltpu.make_async_copy(moe_from, moe_to, sem.at[0]),
        pltpu.make_async_copy(attn_from, attn_to, sem.at[1]),
    ]
    for copy in copies:
        copy.start()
    for copy in copies:
        copy.wait()


def local_fused(
    dims,
    moe_in,
    route_ids,
    route_weights,
    w_gate,
    w_up,
    w_down,
    queries,
    cache_latent,
    cache_rope,
    lengths,
):
    ny, nx, nc, nz = dims
    experts = ny * nx * nc * nz
    rows, width = moe_in.shape
    capacity = 2 * rows * route_ids.shape[1] // experts
    hidden = w_gate.shape[2]
    cache, kv = cache_latent.shape[1:]
    heads = queries.shape[1]
    tokens = experts * rows
    chunks = CHUNKS
    cw = width // chunks
    bf16, f32 = jnp.bfloat16, jnp.float32

    def each(shape, extra=0):
        return [
            pltpu.VMEM(shape + (cw + (extra if c == 0 else 0),), bf16) for c in range(chunks)
        ]

    vmem = pl.BlockSpec(memory_space=pltpu.VMEM)
    hbm = pl.BlockSpec(memory_space=pl.ANY)
    moe_out, attn_out = pl.pallas_call(
        functools.partial(fused_kernel, dims, capacity),
        out_shape=(
            jax.ShapeDtypeStruct((rows, width), bf16),
            jax.ShapeDtypeStruct((1, heads, kv), bf16),
        ),
        in_specs=[
            vmem,
            vmem,
            vmem,
            pl.BlockSpec(memory_space=pltpu.SMEM),
            vmem,
            hbm,
            hbm,
            hbm,
            hbm,
            hbm,
        ],
        out_specs=(vmem, vmem),
        scratch_shapes=[
            each((ny, nx, nc, nz, rows), ROUTE_LANES),
            each((ny, nx, nc, nz, rows)),
            each((ny, nx, nz, rows)),
            each((ny, nx, nz, rows)),
            each((2, nz, rows)),
            each((2, nz, rows)),
            each((nz, rows)),
            each((nz, rows)),
            each((nz - 1, rows)),
            pltpu.VMEM((width, hidden), bf16),
            pltpu.VMEM((width, hidden), bf16),
            pltpu.VMEM((chunks, hidden, cw), bf16),
            pltpu.VMEM((cache, kv), bf16),
            pltpu.VMEM(cache_rope.shape[1:], bf16),
            pltpu.VMEM((cache, heads), f32),
            pltpu.VMEM((heads, kv), f32),
            pltpu.VMEM((experts * capacity, hidden), f32),
            pltpu.VMEM((experts * capacity, hidden), f32),
            pltpu.VMEM((experts * capacity, tokens), bf16),
            pltpu.VMEM((tokens, experts * capacity), bf16),
            pltpu.SemaphoreType.DMA((3, chunks)),
            pltpu.SemaphoreType.DMA((2,)),
            pltpu.SemaphoreType.DMA((chunks, nz + 2)),
            pltpu.SemaphoreType.DMA((chunks, nz + 2)),
            pltpu.SemaphoreType.DMA((chunks, nz + 2)),
            pltpu.SemaphoreType.DMA((chunks, nz + 2)),
        ],
        compiler_params=pltpu.CompilerParams(
            collective_id=0, has_side_effects=True, vmem_limit_bytes=VMEM_BYTES
        ),
        name="fused_moe_attention",
    )(
        moe_in,
        jnp.transpose(route_ids),
        jnp.transpose(route_weights),
        lengths,
        jnp.transpose(queries, (0, 2, 1)),
        w_gate,
        w_up,
        w_down,
        cache_latent,
        cache_rope,
    )
    return pl.pallas_call(
        hand_on,
        out_shape=(
            jax.ShapeDtypeStruct(moe_out.shape, bf16),
            jax.ShapeDtypeStruct(attn_out.shape, bf16),
        ),
        in_specs=[pl.BlockSpec(memory_space=pltpu.HBM)] * 2,
        out_specs=(pl.BlockSpec(memory_space=pltpu.HBM),) * 2,
        scratch_shapes=[pltpu.SemaphoreType.DMA((2,))],
        compiler_params=pltpu.CompilerParams(vmem_limit_bytes=VMEM_BYTES),
        name="hand_on",
    )(moe_out, attn_out)


def solution(mesh):
    placed = (
        P(("node", "local"), None),
        P(("node", "local"), None),
        P(("node", "local"), None),
        P(("node", "local"), None, None),
        P(("node", "local"), None, None),
        P(("node", "local"), None, None),
        P(("node", "local"), None, None),
        P(("node", "local"), None, None),
        P(("node", "local"), None, None),
        P(("node", "local")),
    )
    if mesh.shape["node"] == 8 and mesh.shape["local"] == 4:
        local = functools.partial(local_fused, (2, 2, 2, 4))
    else:
        local = local_general
    return jax.shard_map(
        local,
        mesh=mesh,
        in_specs=placed,
        out_specs=(P(("node", "local"), None), P(("node", "local"), None, None)),
        check_vma=False,
    )
```

```python
import functools

import jax
import jax.numpy as jnp
from jax import lax
from jax.experimental import pallas as pl
from jax.experimental.pallas import tpu as pltpu
from jax.sharding import PartitionSpec as P

score_scale = 192.0 ** (-0.5)
MESH = pl.DeviceIdType.MESH
ROUTE_LANES = 128
ATT_PIECES = 4
IN_STEPS = 7
OUT_LAGS = (0, 1, 3, 5, 8)
CHUNKS = 14
VMEM_BYTES = 60 * 1024 * 1024


def expert_block(block, gate_one, up_one, down_one):
    model_width = block.shape[-1]
    rows_flat = block.reshape(-1, model_width)
    gate_act = jnp.dot(rows_flat, gate_one, preferred_element_type=jnp.float32)
    up_act = jnp.dot(rows_flat, up_one, preferred_element_type=jnp.float32)
    hidden_act = (jax.nn.silu(gate_act) * up_act).astype(jnp.bfloat16)
    result = jnp.dot(hidden_act, down_one, preferred_element_type=jnp.float32).astype(jnp.bfloat16)
    return result.reshape(block.shape)


def attention(queries, cache_latent, cache_rope, lengths):
    kv_width = cache_latent.shape[-1]
    scores = jnp.einsum(
        "rhc,rkc->rhk", queries[:, :, :kv_width], cache_latent, preferred_element_type=jnp.float32
    )
    scores = (
        scores
        + jnp.einsum(
            "rhc,rck->rhk", queries[:, :, kv_width:], cache_rope, preferred_element_type=jnp.float32
        )
    ) * score_scale
    positions = jnp.arange(cache_latent.shape[1], dtype=jnp.int32)
    scores = jnp.where(positions[None, None, :] < lengths[:, None, None], scores, -jnp.inf)
    peak = jnp.max(scores, axis=-1, keepdims=True)
    weights = jnp.exp(scores - peak)
    probs = (weights / jnp.sum(weights, axis=-1, keepdims=True)).astype(jnp.bfloat16)
    return jnp.einsum(
        "rhk,rkc->rhc", probs, cache_latent, preferred_element_type=jnp.float32
    ).astype(jnp.bfloat16)


def local_general(
    moe_in,
    route_ids,
    route_weights,
    w_gate,
    w_up,
    w_down,
    queries,
    cache_latent,
    cache_rope,
    lengths,
):
    attn_out = attention(queries, cache_latent, cache_rope, lengths)
    expert_count = lax.axis_size("node") * lax.axis_size("local")
    row_count, model_width = moe_in.shape
    top_count = route_ids.shape[1]
    capacity = 2 * row_count * top_count // expert_count
    row_index = jnp.broadcast_to(jnp.arange(row_count, dtype=jnp.int32)[:, None], route_ids.shape)
    padded = jnp.concatenate([moe_in, jnp.zeros((1, model_width), moe_in.dtype)], axis=0)
    expert_hits = (
        route_ids[:, :, None] == jnp.arange(expert_count, dtype=jnp.int32)[None, None, :]
    ).astype(jnp.int32)
    present = jnp.sum(expert_hits, axis=1, dtype=jnp.int32)
    earlier = jnp.cumsum(present, axis=0, dtype=jnp.int32) - present
    rank_of = jnp.sum(expert_hits * earlier[:, None, :], axis=-1, dtype=jnp.int32)
    slot_of = route_ids * capacity + rank_of
    table = (
        jnp.full((expert_count * capacity,), row_count, jnp.int32)
        .at[slot_of.reshape(-1)]
        .set(row_index.reshape(-1))
    )
    outgoing = padded[table].reshape(expert_count, capacity, model_width)
    result = expert_block(
        lax.all_to_all(outgoing, ("node", "local"), split_axis=0, concat_axis=0, tiled=True),
        w_gate[0],
        w_up[0],
        w_down[0],
    )
    returned = lax.all_to_all(result, ("node", "local"), split_axis=0, concat_axis=0, tiled=True)
    picked = returned.reshape(expert_count * capacity, model_width)[slot_of]
    total = jnp.einsum("rk,rkd->rd", route_weights, picked.astype(jnp.float32))
    return (total.astype(jnp.bfloat16), attn_out)


def fused_kernel(
    dims,
    capacity,
    x_ref,
    ids_ref,
    rw_ref,
    len_ref,
    q_ref,
    gate_hbm,
    up_hbm,
    down_hbm,
    latent_hbm,
    rope_hbm,
    moe_ref,
    attn_ref,
    gathered,
    part,
    recv_core,
    sum_core,
    recv_one,
    sum_one,
    recv_two,
    sum_two,
    recv_z,
    gate_w,
    up_w,
    down_w,
    latent,
    rope,
    scores,
    attn_acc,
    gate_acc,
    up_acc,
    pick,
    spread,
    load_sem,
    cache_sem,
    ag_send,
    ag_recv,
    rs_send,
    rs_recv,
):
    ny, nx, nc, nz = dims
    rows, width = x_ref.shape
    chunks = len(gathered)
    cw = width // chunks
    merge = chunks // IN_STEPS
    tokens = ny * nx * nc * nz * rows
    slots_total = ny * nx * nc * nz * capacity
    hidden = gate_w.shape[1]
    f32, bf16 = jnp.float32, jnp.bfloat16

    node = lax.axis_index("node")
    z = lax.axis_index("local")
    core = lax.rem(node, nc)
    x = lax.rem(node // nc, nx)
    y = node // (nc * nx)
    me = node * nz + z

    def device(yy, xx, cc, zz):
        return ((yy * nx + xx) * nc + cc, zz)

    core_dev = device(y, x, 1 - core, z)
    x_dev = device(y, 1 - x, core, z)
    y_dev = device(1 - y, x, core, z)
    z_at = [lax.rem(z + o, nz) for o in range(nz)]
    z_devs = [device(y, x, core, z_at[o]) for o in range(1, nz)]

    barrier = pltpu.get_barrier_semaphore()
    for dev in [core_dev, x_dev, y_dev] + z_devs:
        pl.semaphore_signal(barrier, inc=1, device_id=dev, device_id_type=MESH)

    cache_loads = [
        pltpu.make_async_copy(latent_hbm.at[0], latent, cache_sem.at[0]),
        pltpu.make_async_copy(rope_hbm.at[0], rope, cache_sem.at[1]),
    ]
    for load in cache_loads:
        load.start()
    gate_loads, up_loads, down_loads = [], [], []
    for m in range(chunks // merge):
        at = pl.ds(m * merge * cw, merge * cw)
        gate_loads.append(
            pltpu.make_async_copy(gate_hbm.at[0, at], gate_w.at[at], load_sem.at[0, m])
        )
        up_loads.append(pltpu.make_async_copy(up_hbm.at[0, at], up_w.at[at], load_sem.at[1, m]))
    for c in range(chunks):
        at = pl.ds(c * cw, cw)
        down_loads.append(
            pltpu.make_async_copy(down_hbm.at[0, :, at], down_w.at[c], load_sem.at[2, c])
        )

    lanes = lax.broadcasted_iota(jnp.int32, (rows, ROUTE_LANES), 1)
    ids = jnp.transpose(ids_ref[...])
    rw = jnp.transpose(rw_ref[...])
    table = jnp.zeros((rows, ROUTE_LANES), f32)
    for k in range(ids.shape[1]):
        table = table + jnp.where(lanes == ids[:, k : k + 1], rw[:, k : k + 1], 0.0)
    gathered[0][y, x, core, z, :, :ROUTE_LANES] = table.astype(bf16)
    gathered[0][y, x, core, z, :, ROUTE_LANES:] = x_ref[:, :cw]
    for c in range(1, chunks):
        gathered[c][y, x, core, z] = x_ref[:, c * cw : (c + 1) * cw]

    pl.semaphore_wait(barrier, 2 + nz)

    sends = []

    def push(src, dst, send_sem, recv_sem, dev):
        copy = pltpu.make_async_remote_copy(
            src_ref=src,
            dst_ref=dst,
            send_sem=send_sem,
            recv_sem=recv_sem,
            device_id=dev,
            device_id_type=MESH,
        )
        copy.start()
        sends.append(copy)

    def arrived(dst, send_sem, recv_sem, dev):
        pltpu.make_async_remote_copy(
            src_ref=dst,
            dst_ref=dst,
            send_sem=send_sem,
            recv_sem=recv_sem,
            device_id=dev,
            device_id_type=MESH,
        ).wait_recv()

    def gather_z(c):
        own = gathered[c].at[y, x, core, z]
        for o in range(1, nz):
            push(own, own, ag_send.at[c, o - 1], ag_recv.at[c, o - 1], z_devs[o - 1])

    def gather_z_wait(c):
        for o in range(1, nz):
            arrived(
                gathered[c].at[y, x, core, z_at[nz - o]],
                ag_send.at[c, o - 1],
                ag_recv.at[c, o - 1],
                z_devs[nz - o - 1],
            )

    def gather_views(c):
        first = gathered[c].at[y, x, core]
        if c % 2 == 0:
            return [
                (first, gathered[c].at[y, 1 - x, core], x_dev),
                (gathered[c].at[y, :, core], gathered[c].at[1 - y, :, core], y_dev),
                (gathered[c].at[:, :, core], gathered[c].at[:, :, 1 - core], core_dev),
            ]
        return [
            (first, gathered[c].at[1 - y, x, core], y_dev),
            (gathered[c].at[:, x, core], gathered[c].at[:, 1 - x, core], x_dev),
            (gathered[c].at[:, :, core], gathered[c].at[:, :, 1 - core], core_dev),
        ]

    def gather_push(c, phase):
        src, _, dev = gather_views(c)[phase]
        k = nz - 1 + phase
        push(src, src, ag_send.at[c, k], ag_recv.at[c, k], dev)

    def gather_wait(c, phase):
        _, dst, dev = gather_views(c)[phase]
        k = nz - 1 + phase
        arrived(dst, ag_send.at[c, k], ag_recv.at[c, k], dev)

    kv = latent.shape[1]
    cache = latent.shape[0]
    piece = cache // ATT_PIECES
    length = len_ref[0]

    def score_piece(i):
        at = slice(i * piece, (i + 1) * piece)
        s = jnp.dot(latent[at, :], q_ref[0, :kv, :], preferred_element_type=f32)
        s = s + lax.dot_general(
            rope[:, at], q_ref[0, kv:, :], (((0,), (0,)), ((), ())), preferred_element_type=f32
        )
        positions = lax.broadcasted_iota(jnp.int32, s.shape, 0) + i * piece
        scores[at, :] = jnp.where(positions < length, s * score_scale, -jnp.inf)

    def soft():
        s = scores[...]
        e = jnp.exp(s - jnp.max(s, axis=0, keepdims=True))
        scores[...] = e / jnp.sum(e, axis=0, keepdims=True)

    def value_piece(i):
        at = slice(i * piece, (i + 1) * piece)
        got = lax.dot_general(
            scores[at, :].astype(bf16),
            latent[at, :],
            (((0,), (0,)), ((), ())),
            preferred_element_type=f32,
        )
        if i == 0:
            attn_acc[...] = got
        elif i < ATT_PIECES - 1:
            attn_acc[...] += got
        else:
            attn_ref[0] = (attn_acc[...] + got).astype(bf16)

    def first_piece():
        for load in cache_loads:
            load.wait()
        score_piece(0)

    tasks = [first_piece]
    tasks += [functools.partial(score_piece, i) for i in range(1, ATT_PIECES)]
    tasks += [soft]
    tasks += [functools.partial(value_piece, i) for i in range(ATT_PIECES)]

    def route():
        sent = gathered[0][:, :, :, :, :, :ROUTE_LANES].reshape(tokens, ROUTE_LANES)
        mine = (lax.broadcasted_iota(jnp.int32, (16, ROUTE_LANES), 1) == me).astype(bf16)
        weight = lax.dot_general(
            mine, sent, (((1,), (1,)), ((), ())), preferred_element_type=f32
        )
        present = weight > 0.0
        t_from = lax.broadcasted_iota(jnp.int32, (tokens, tokens), 0)
        t_to = lax.broadcasted_iota(jnp.int32, (tokens, tokens), 1)
        before = ((t_from < t_to) & (t_from // rows == t_to // rows)).astype(bf16)
        rank = jnp.dot(present.astype(bf16), before, preferred_element_type=f32)
        base = (lax.broadcasted_iota(jnp.int32, (16, tokens), 1) // rows) * capacity
        slot = jnp.where(present, rank + base.astype(f32), -1.0)
        slot_id = lax.broadcasted_iota(jnp.int32, (slots_total, tokens), 0).astype(f32)
        hit = slot[0:1, :] == slot_id
        pick[...] = hit.astype(bf16)
        spread[...] = jnp.transpose(jnp.where(hit, weight[0:1, :], 0.0)).astype(bf16)

    def expert_in(m):
        picked = []
        for c in range(m * merge, (m + 1) * merge):
            g = gathered[c][...] if c else gathered[c][:, :, :, :, :, ROUTE_LANES:]
            picked.append(
                jnp.dot(pick[...], g.reshape(tokens, cw), preferred_element_type=f32).astype(bf16)
            )
        rows_in = picked[0] if merge == 1 else jnp.concatenate(picked, axis=1)
        gate_loads[m].wait()
        up_loads[m].wait()
        at = slice(m * merge * cw, (m + 1) * merge * cw)
        for acc, w in ((gate_acc, gate_w), (up_acc, up_w)):
            got = jnp.dot(rows_in, w[at, :], preferred_element_type=f32)
            if m == 0:
                acc[...] = got
            else:
                acc[...] += got

    for c in range(chunks):
        gather_z(c)
    for m in range(chunks // merge):
        gate_loads[m].start()
        up_loads[m].start()
    for c in range(chunks):
        down_loads[c].start()
    for s in range(chunks + 6):
        if s < chunks:
            gather_z_wait(s)
            gather_push(s, 0)
        for phase in range(2):
            c = s - 2 - 2 * phase
            if 0 <= c < chunks:
                gather_wait(c, phase)
                gather_push(c, phase + 1)
        for _ in range(2 if s < 4 else 1):
            if tasks:
                tasks.pop(0)()
        c = s - 6
        if 0 <= c < chunks:
            gather_wait(c, 2)
            if c == 0:
                route()
            if c % merge == merge - 1:
                expert_in(c // merge)
    for task in tasks:
        task()

    gate = gate_acc[...]
    hidden_act = (gate / (1.0 + jnp.exp(-gate)) * up_acc[...]).astype(bf16)

    def add_to(dst, a, b):
        dst[...] = (a.astype(f32) + b.astype(f32)).astype(bf16)

    def out_views(c):
        if c % 2 == 0:
            return [
                (part[c].at[:, :, 1 - core], recv_core[c], core_dev),
                (sum_core[c].at[1 - y], recv_one[c], y_dev),
                (sum_one[c].at[1 - x], recv_two[c], x_dev),
            ]
        return [
            (part[c].at[:, :, 1 - core], recv_core[c], core_dev),
            (sum_core[c].at[:, 1 - x], recv_one[c], x_dev),
            (sum_one[c].at[1 - y], recv_two[c], y_dev),
        ]

    def out_push(c, phase):
        src, dst, dev = out_views(c)[phase]
        push(src, dst, rs_send.at[c, phase], rs_recv.at[c, phase], dev)

    def out_wait(c, phase):
        _, dst, dev = out_views(c)[phase]
        arrived(dst, rs_send.at[c, phase], rs_recv.at[c, phase], dev)

    def stage_zero(c):
        down_loads[c].wait()
        out = jnp.dot(hidden_act, down_w[c], preferred_element_type=f32).astype(bf16)
        got = jnp.dot(spread[...], out, preferred_element_type=f32).astype(bf16)
        part[c][...] = got.reshape(part[c].shape)
        out_push(c, 0)

    def stage_one(c):
        out_wait(c, 0)
        add_to(sum_core[c], part[c][:, :, core], recv_core[c][...])
        out_push(c, 1)

    def stage_two(c):
        out_wait(c, 1)
        kept = sum_core[c][y] if c % 2 == 0 else sum_core[c][:, x]
        add_to(sum_one[c], kept, recv_one[c][...])
        out_push(c, 2)

    def stage_three(c):
        out_wait(c, 2)
        kept = sum_one[c][x] if c % 2 == 0 else sum_one[c][y]
        add_to(sum_two[c], kept, recv_two[c][...])
        for o in range(1, nz):
            push(
                sum_two[c].at[z_at[o]],
                recv_z[c].at[o - 1],
                rs_send.at[c, 2 + o],
                rs_recv.at[c, 2 + o],
                z_devs[o - 1],
            )

    def stage_four(c):
        total = sum_two[c][z].astype(f32)
        for o in range(1, nz):
            arrived(
                recv_z[c].at[o - 1], rs_send.at[c, 2 + o], rs_recv.at[c, 2 + o], z_devs[nz - o - 1]
            )
            total = total + recv_z[c][o - 1].astype(f32)
        moe_ref[:, c * cw : (c + 1) * cw] = total.astype(bf16)

    stages = [stage_zero, stage_one, stage_two, stage_three, stage_four]
    for s in range(chunks + OUT_LAGS[-1]):
        for lag, stage in zip(OUT_LAGS, stages):
            c = s - lag
            if 0 <= c < chunks:
                stage(c)

    for copy in sends:
        copy.wait_send()


def local_fused(
    dims,
    moe_in,
    route_ids,
    route_weights,
    w_gate,
    w_up,
    w_down,
    queries,
    cache_latent,
    cache_rope,
    lengths,
):
    ny, nx, nc, nz = dims
    experts = ny * nx * nc * nz
    rows, width = moe_in.shape
    capacity = 2 * rows * route_ids.shape[1] // experts
    hidden = w_gate.shape[2]
    cache, kv = cache_latent.shape[1:]
    heads = queries.shape[1]
    tokens = experts * rows
    chunks = CHUNKS
    cw = width // chunks
    bf16, f32 = jnp.bfloat16, jnp.float32

    def each(shape, extra=0):
        return [
            pltpu.VMEM(shape + (cw + (extra if c == 0 else 0),), bf16) for c in range(chunks)
        ]

    vmem = pl.BlockSpec(memory_space=pltpu.VMEM)
    hbm = pl.BlockSpec(memory_space=pl.ANY)
    moe_out, attn_out = pl.pallas_call(
        functools.partial(fused_kernel, dims, capacity),
        out_shape=(
            jax.ShapeDtypeStruct((rows, width), bf16),
            jax.ShapeDtypeStruct((1, heads, kv), bf16),
        ),
        in_specs=[
            vmem,
            vmem,
            vmem,
            pl.BlockSpec(memory_space=pltpu.SMEM),
            vmem,
            hbm,
            hbm,
            hbm,
            hbm,
            hbm,
        ],
        out_specs=(vmem, vmem),
        scratch_shapes=[
            each((ny, nx, nc, nz, rows), ROUTE_LANES),
            each((ny, nx, nc, nz, rows)),
            each((ny, nx, nz, rows)),
            each((ny, nx, nz, rows)),
            each((2, nz, rows)),
            each((2, nz, rows)),
            each((nz, rows)),
            each((nz, rows)),
            each((nz - 1, rows)),
            pltpu.VMEM((width, hidden), bf16),
            pltpu.VMEM((width, hidden), bf16),
            pltpu.VMEM((chunks, hidden, cw), bf16),
            pltpu.VMEM((cache, kv), bf16),
            pltpu.VMEM(cache_rope.shape[1:], bf16),
            pltpu.VMEM((cache, heads), f32),
            pltpu.VMEM((heads, kv), f32),
            pltpu.VMEM((experts * capacity, hidden), f32),
            pltpu.VMEM((experts * capacity, hidden), f32),
            pltpu.VMEM((experts * capacity, tokens), bf16),
            pltpu.VMEM((tokens, experts * capacity), bf16),
            pltpu.SemaphoreType.DMA((3, chunks)),
            pltpu.SemaphoreType.DMA((2,)),
            pltpu.SemaphoreType.DMA((chunks, nz + 2)),
            pltpu.SemaphoreType.DMA((chunks, nz + 2)),
            pltpu.SemaphoreType.DMA((chunks, nz + 2)),
            pltpu.SemaphoreType.DMA((chunks, nz + 2)),
        ],
        compiler_params=pltpu.CompilerParams(
            collective_id=0, has_side_effects=True, vmem_limit_bytes=VMEM_BYTES
        ),
        name="fused_moe_attention",
    )(
        moe_in,
        jnp.transpose(route_ids),
        jnp.transpose(route_weights),
        lengths,
        jnp.transpose(queries, (0, 2, 1)),
        w_gate,
        w_up,
        w_down,
        cache_latent,
        cache_rope,
    )
    return moe_out, attn_out


def solution(mesh):
    placed = (
        P(("node", "local"), None),
        P(("node", "local"), None),
        P(("node", "local"), None),
        P(("node", "local"), None, None),
        P(("node", "local"), None, None),
        P(("node", "local"), None, None),
        P(("node", "local"), None, None),
        P(("node", "local"), None, None),
        P(("node", "local"), None, None),
        P(("node", "local")),
    )
    if mesh.shape["node"] == 8 and mesh.shape["local"] == 4:
        local = functools.partial(local_fused, (2, 2, 2, 4))
    else:
        local = local_general
    return jax.shard_map(
        local,
        mesh=mesh,
        in_specs=placed,
        out_specs=(P(("node", "local"), None), P(("node", "local"), None, None)),
        check_vma=False,
    )
```

```python
import functools

import jax
import jax.numpy as jnp
from jax import lax
from jax.experimental import pallas as pl
from jax.experimental.pallas import tpu as pltpu
from jax.sharding import PartitionSpec as P

score_scale = 192.0 ** (-0.5)
MESH = pl.DeviceIdType.MESH
ROUTE_LANES = 128
ATT_PIECES = 4
IN_STEPS = 7
OUT_LAGS = (0, 1, 2, 3, 4)
CHUNKS = 7
VMEM_BYTES = 60 * 1024 * 1024


def expert_block(block, gate_one, up_one, down_one):
    model_width = block.shape[-1]
    rows_flat = block.reshape(-1, model_width)
    gate_act = jnp.dot(rows_flat, gate_one, preferred_element_type=jnp.float32)
    up_act = jnp.dot(rows_flat, up_one, preferred_element_type=jnp.float32)
    hidden_act = (jax.nn.silu(gate_act) * up_act).astype(jnp.bfloat16)
    result = jnp.dot(hidden_act, down_one, preferred_element_type=jnp.float32).astype(jnp.bfloat16)
    return result.reshape(block.shape)


def attention(queries, cache_latent, cache_rope, lengths):
    kv_width = cache_latent.shape[-1]
    scores = jnp.einsum(
        "rhc,rkc->rhk", queries[:, :, :kv_width], cache_latent, preferred_element_type=jnp.float32
    )
    scores = (
        scores
        + jnp.einsum(
            "rhc,rck->rhk", queries[:, :, kv_width:], cache_rope, preferred_element_type=jnp.float32
        )
    ) * score_scale
    positions = jnp.arange(cache_latent.shape[1], dtype=jnp.int32)
    scores = jnp.where(positions[None, None, :] < lengths[:, None, None], scores, -jnp.inf)
    peak = jnp.max(scores, axis=-1, keepdims=True)
    weights = jnp.exp(scores - peak)
    probs = (weights / jnp.sum(weights, axis=-1, keepdims=True)).astype(jnp.bfloat16)
    return jnp.einsum(
        "rhk,rkc->rhc", probs, cache_latent, preferred_element_type=jnp.float32
    ).astype(jnp.bfloat16)


def local_general(
    moe_in,
    route_ids,
    route_weights,
    w_gate,
    w_up,
    w_down,
    queries,
    cache_latent,
    cache_rope,
    lengths,
):
    attn_out = attention(queries, cache_latent, cache_rope, lengths)
    expert_count = lax.axis_size("node") * lax.axis_size("local")
    row_count, model_width = moe_in.shape
    top_count = route_ids.shape[1]
    capacity = 2 * row_count * top_count // expert_count
    row_index = jnp.broadcast_to(jnp.arange(row_count, dtype=jnp.int32)[:, None], route_ids.shape)
    padded = jnp.concatenate([moe_in, jnp.zeros((1, model_width), moe_in.dtype)], axis=0)
    expert_hits = (
        route_ids[:, :, None] == jnp.arange(expert_count, dtype=jnp.int32)[None, None, :]
    ).astype(jnp.int32)
    present = jnp.sum(expert_hits, axis=1, dtype=jnp.int32)
    earlier = jnp.cumsum(present, axis=0, dtype=jnp.int32) - present
    rank_of = jnp.sum(expert_hits * earlier[:, None, :], axis=-1, dtype=jnp.int32)
    slot_of = route_ids * capacity + rank_of
    table = (
        jnp.full((expert_count * capacity,), row_count, jnp.int32)
        .at[slot_of.reshape(-1)]
        .set(row_index.reshape(-1))
    )
    outgoing = padded[table].reshape(expert_count, capacity, model_width)
    result = expert_block(
        lax.all_to_all(outgoing, ("node", "local"), split_axis=0, concat_axis=0, tiled=True),
        w_gate[0],
        w_up[0],
        w_down[0],
    )
    returned = lax.all_to_all(result, ("node", "local"), split_axis=0, concat_axis=0, tiled=True)
    picked = returned.reshape(expert_count * capacity, model_width)[slot_of]
    total = jnp.einsum("rk,rkd->rd", route_weights, picked.astype(jnp.float32))
    return (total.astype(jnp.bfloat16), attn_out)


def fused_kernel(
    dims,
    capacity,
    x_ref,
    ids_ref,
    rw_ref,
    len_ref,
    q_ref,
    gate_hbm,
    up_hbm,
    down_hbm,
    latent_hbm,
    rope_hbm,
    moe_ref,
    attn_ref,
    gathered,
    part,
    recv_core,
    sum_core,
    recv_one,
    sum_one,
    recv_two,
    sum_two,
    recv_z,
    gate_w,
    up_w,
    down_w,
    latent,
    rope,
    scores,
    attn_acc,
    gate_acc,
    up_acc,
    pick,
    spread,
    load_sem,
    cache_sem,
    ag_send,
    ag_recv,
    rs_send,
    rs_recv,
):
    ny, nx, nc, nz = dims
    rows, width = x_ref.shape
    chunks = len(gathered)
    cw = width // chunks
    merge = chunks // IN_STEPS
    tokens = ny * nx * nc * nz * rows
    slots_total = ny * nx * nc * nz * capacity
    hidden = gate_w.shape[1]
    f32, bf16 = jnp.float32, jnp.bfloat16

    node = lax.axis_index("node")
    z = lax.axis_index("local")
    core = lax.rem(node, nc)
    x = lax.rem(node // nc, nx)
    y = node // (nc * nx)
    me = node * nz + z

    def device(yy, xx, cc, zz):
        return ((yy * nx + xx) * nc + cc, zz)

    p = y + core * (x - y)
    q = x + core * (y - x)
    core_dev = device(y, x, 1 - core, z)
    p_dev = device(y + (1 - core) * (1 - 2 * y), x + core * (1 - 2 * x), core, z)
    q_dev = device(y + core * (1 - 2 * y), x + (1 - core) * (1 - 2 * x), core, z)
    z_at = [lax.rem(z + o, nz) for o in range(nz)]
    z_devs = [device(y, x, core, z_at[o]) for o in range(1, nz)]

    barrier = pltpu.get_barrier_semaphore()
    for dev in [core_dev, p_dev, q_dev] + z_devs:
        pl.semaphore_signal(barrier, inc=1, device_id=dev, device_id_type=MESH)

    cache_loads = [
        pltpu.make_async_copy(latent_hbm.at[0], latent, cache_sem.at[0]),
        pltpu.make_async_copy(rope_hbm.at[0], rope, cache_sem.at[1]),
    ]
    for load in cache_loads:
        load.start()
    gate_loads, up_loads, down_loads = [], [], []
    for m in range(chunks // merge):
        at = pl.ds(m * merge * cw, merge * cw)
        gate_loads.append(
            pltpu.make_async_copy(gate_hbm.at[0, at], gate_w.at[at], load_sem.at[0, m])
        )
        up_loads.append(pltpu.make_async_copy(up_hbm.at[0, at], up_w.at[at], load_sem.at[1, m]))
    for c in range(chunks):
        at = pl.ds(c * cw, cw)
        down_loads.append(
            pltpu.make_async_copy(down_hbm.at[0, :, at], down_w.at[c], load_sem.at[2, c])
        )
    for m in range(chunks // merge):
        gate_loads[m].start()
        up_loads[m].start()
    for c in range(chunks):
        down_loads[c].start()

    lanes = lax.broadcasted_iota(jnp.int32, (rows, ROUTE_LANES), 1)
    ids = jnp.transpose(ids_ref[...])
    rw = jnp.transpose(rw_ref[...])
    table = jnp.zeros((rows, ROUTE_LANES), f32)
    for k in range(ids.shape[1]):
        table = table + jnp.where(lanes == ids[:, k : k + 1], rw[:, k : k + 1], 0.0)
    gathered[0][core, p, q, z, :, :ROUTE_LANES] = table.astype(bf16)
    gathered[0][core, p, q, z, :, ROUTE_LANES:] = x_ref[:, :cw]
    for c in range(1, chunks):
        gathered[c][core, p, q, z] = x_ref[:, c * cw : (c + 1) * cw]

    pl.semaphore_wait(barrier, 2 + nz)

    sends = []

    def push(src, dst, send_sem, recv_sem, dev):
        copy = pltpu.make_async_remote_copy(
            src_ref=src,
            dst_ref=dst,
            send_sem=send_sem,
            recv_sem=recv_sem,
            device_id=dev,
            device_id_type=MESH,
        )
        copy.start()
        sends.append(copy)

    def arrived(dst, send_sem, recv_sem, dev):
        pltpu.make_async_remote_copy(
            src_ref=dst,
            dst_ref=dst,
            send_sem=send_sem,
            recv_sem=recv_sem,
            device_id=dev,
            device_id_type=MESH,
        ).wait_recv()

    def gather_z(c):
        own = gathered[c].at[core, p, q, z]
        for o in range(1, nz):
            push(own, own, ag_send.at[c, o - 1], ag_recv.at[c, o - 1], z_devs[o - 1])

    def gather_z_wait(c):
        for o in range(1, nz):
            arrived(
                gathered[c].at[core, p, q, z_at[nz - o]],
                ag_send.at[c, o - 1],
                ag_recv.at[c, o - 1],
                z_devs[nz - o - 1],
            )

    def gather_views(c):
        g = gathered[c]
        return [
            (g.at[core, p, q], g.at[core, p, 1 - q], q_dev),
            (g.at[core, p], g.at[core, 1 - p], p_dev),
            (g.at[core], g.at[1 - core], core_dev),
        ]

    def gather_push(c, phase):
        src, _, dev = gather_views(c)[phase]
        k = nz - 1 + phase
        push(src, src, ag_send.at[c, k], ag_recv.at[c, k], dev)

    def gather_wait(c, phase):
        _, dst, dev = gather_views(c)[phase]
        k = nz - 1 + phase
        arrived(dst, ag_send.at[c, k], ag_recv.at[c, k], dev)

    kv = latent.shape[1]
    cache = latent.shape[0]
    piece = cache // ATT_PIECES
    length = len_ref[0]

    def score_piece(i):
        at = slice(i * piece, (i + 1) * piece)
        s = jnp.dot(latent[at, :], q_ref[0, :kv, :], preferred_element_type=f32)
        s = s + lax.dot_general(
            rope[:, at], q_ref[0, kv:, :], (((0,), (0,)), ((), ())), preferred_element_type=f32
        )
        positions = lax.broadcasted_iota(jnp.int32, s.shape, 0) + i * piece
        scores[at, :] = jnp.where(positions < length, s * score_scale, -jnp.inf)

    def soft():
        s = scores[...]
        e = jnp.exp(s - jnp.max(s, axis=0, keepdims=True))
        scores[...] = e / jnp.sum(e, axis=0, keepdims=True)

    def value_piece(i):
        at = slice(i * piece, (i + 1) * piece)
        got = lax.dot_general(
            scores[at, :].astype(bf16),
            latent[at, :],
            (((0,), (0,)), ((), ())),
            preferred_element_type=f32,
        )
        if i == 0:
            attn_acc[...] = got
        elif i < ATT_PIECES - 1:
            attn_acc[...] += got
        else:
            attn_ref[0] = (attn_acc[...] + got).astype(bf16)

    def first_piece():
        for load in cache_loads:
            load.wait()
        score_piece(0)

    tasks = [first_piece]
    tasks += [functools.partial(score_piece, i) for i in range(1, ATT_PIECES)]
    tasks += [soft]
    tasks += [functools.partial(value_piece, i) for i in range(ATT_PIECES)]

    def route():
        sent = gathered[0][:, :, :, :, :, :ROUTE_LANES].reshape(tokens, ROUTE_LANES)
        mine = (lax.broadcasted_iota(jnp.int32, (16, ROUTE_LANES), 1) == me).astype(bf16)
        weight = lax.dot_general(
            mine, sent, (((1,), (1,)), ((), ())), preferred_element_type=f32
        )
        present = weight > 0.0
        t_from = lax.broadcasted_iota(jnp.int32, (tokens, tokens), 0)
        t_to = lax.broadcasted_iota(jnp.int32, (tokens, tokens), 1)
        before = ((t_from < t_to) & (t_from // rows == t_to // rows)).astype(bf16)
        rank = jnp.dot(present.astype(bf16), before, preferred_element_type=f32)
        base = (lax.broadcasted_iota(jnp.int32, (16, tokens), 1) // rows) * capacity
        slot = jnp.where(present, rank + base.astype(f32), -1.0)
        slot_id = lax.broadcasted_iota(jnp.int32, (slots_total, tokens), 0).astype(f32)
        hit = slot[0:1, :] == slot_id
        pick[...] = hit.astype(bf16)
        spread[...] = jnp.transpose(jnp.where(hit, weight[0:1, :], 0.0)).astype(bf16)

    def expert_in(m):
        picked = []
        for c in range(m * merge, (m + 1) * merge):
            g = gathered[c][...] if c else gathered[c][:, :, :, :, :, ROUTE_LANES:]
            picked.append(
                jnp.dot(pick[...], g.reshape(tokens, cw), preferred_element_type=f32).astype(bf16)
            )
        rows_in = picked[0] if merge == 1 else jnp.concatenate(picked, axis=1)
        gate_loads[m].wait()
        up_loads[m].wait()
        at = slice(m * merge * cw, (m + 1) * merge * cw)
        for acc, w in ((gate_acc, gate_w), (up_acc, up_w)):
            got = jnp.dot(rows_in, w[at, :], preferred_element_type=f32)
            if m == 0:
                acc[...] = got
            else:
                acc[...] += got

    for c in range(chunks):
        gather_z(c)
    for s in range(chunks + 3):
        if s < chunks:
            gather_z_wait(s)
            gather_push(s, 0)
        for phase in range(2):
            c = s - 1 - phase
            if 0 <= c < chunks:
                gather_wait(c, phase)
                gather_push(c, phase + 1)
        for _ in range(2 if s < 3 else 1):
            if tasks:
                tasks.pop(0)()
        c = s - 3
        if 0 <= c < chunks:
            gather_wait(c, 2)
            if c == 0:
                route()
            if c % merge == merge - 1:
                expert_in(c // merge)
    for task in tasks:
        task()

    gate = gate_acc[...]
    hidden_act = (gate / (1.0 + jnp.exp(-gate)) * up_acc[...]).astype(bf16)

    def add_to(dst, a, b):
        dst[...] = (a.astype(f32) + b.astype(f32)).astype(bf16)

    def out_views(c):
        return [
            (part[c].at[1 - core], recv_core[c], core_dev),
            (sum_core[c].at[1 - p], recv_one[c], p_dev),
            (sum_one[c].at[1 - q], recv_two[c], q_dev),
        ]

    def out_push(c, phase):
        src, dst, dev = out_views(c)[phase]
        push(src, dst, rs_send.at[c, phase], rs_recv.at[c, phase], dev)

    def out_wait(c, phase):
        _, dst, dev = out_views(c)[phase]
        arrived(dst, rs_send.at[c, phase], rs_recv.at[c, phase], dev)

    def stage_zero(c):
        down_loads[c].wait()
        out = jnp.dot(hidden_act, down_w[c], preferred_element_type=f32).astype(bf16)
        got = jnp.dot(spread[...], out, preferred_element_type=f32).astype(bf16)
        part[c][...] = got.reshape(part[c].shape)
        out_push(c, 0)

    def stage_one(c):
        out_wait(c, 0)
        add_to(sum_core[c], part[c][core], recv_core[c][...])
        out_push(c, 1)

    def stage_two(c):
        out_wait(c, 1)
        add_to(sum_one[c], sum_core[c][p], recv_one[c][...])
        out_push(c, 2)

    def stage_three(c):
        out_wait(c, 2)
        add_to(sum_two[c], sum_one[c][q], recv_two[c][...])
        for o in range(1, nz):
            push(
                sum_two[c].at[z_at[o]],
                recv_z[c].at[o - 1],
                rs_send.at[c, 2 + o],
                rs_recv.at[c, 2 + o],
                z_devs[o - 1],
            )

    def stage_four(c):
        total = sum_two[c][z].astype(f32)
        for o in range(1, nz):
            arrived(
                recv_z[c].at[o - 1], rs_send.at[c, 2 + o], rs_recv.at[c, 2 + o], z_devs[nz - o - 1]
            )
            total = total + recv_z[c][o - 1].astype(f32)
        moe_ref[:, c * cw : (c + 1) * cw] = total.astype(bf16)

    stages = [stage_zero, stage_one, stage_two, stage_three, stage_four]
    for s in range(chunks + OUT_LAGS[-1]):
        for lag, stage in zip(OUT_LAGS, stages):
            c = s - lag
            if 0 <= c < chunks:
                stage(c)

    for copy in sends:
        copy.wait_send()


def local_fused(
    dims,
    moe_in,
    route_ids,
    route_weights,
    w_gate,
    w_up,
    w_down,
    queries,
    cache_latent,
    cache_rope,
    lengths,
):
    ny, nx, nc, nz = dims
    experts = ny * nx * nc * nz
    rows, width = moe_in.shape
    capacity = 2 * rows * route_ids.shape[1] // experts
    hidden = w_gate.shape[2]
    cache, kv = cache_latent.shape[1:]
    heads = queries.shape[1]
    tokens = experts * rows
    chunks = CHUNKS
    cw = width // chunks
    bf16, f32 = jnp.bfloat16, jnp.float32

    def each(shape, extra=0):
        return [
            pltpu.VMEM(shape + (cw + (extra if c == 0 else 0),), bf16) for c in range(chunks)
        ]

    vmem = pl.BlockSpec(memory_space=pltpu.VMEM)
    hbm = pl.BlockSpec(memory_space=pl.ANY)
    moe_out, attn_out = pl.pallas_call(
        functools.partial(fused_kernel, dims, capacity),
        out_shape=(
            jax.ShapeDtypeStruct((rows, width), bf16),
            jax.ShapeDtypeStruct((1, heads, kv), bf16),
        ),
        in_specs=[
            vmem,
            vmem,
            vmem,
            pl.BlockSpec(memory_space=pltpu.SMEM),
            vmem,
            hbm,
            hbm,
            hbm,
            hbm,
            hbm,
        ],
        out_specs=(vmem, vmem),
        scratch_shapes=[
            each((nc, 2, 2, nz, rows), ROUTE_LANES),
            each((nc, 2, 2, nz, rows)),
            each((2, 2, nz, rows)),
            each((2, 2, nz, rows)),
            each((2, nz, rows)),
            each((2, nz, rows)),
            each((nz, rows)),
            each((nz, rows)),
            each((nz - 1, rows)),
            pltpu.VMEM((width, hidden), bf16),
            pltpu.VMEM((width, hidden), bf16),
            pltpu.VMEM((chunks, hidden, cw), bf16),
            pltpu.VMEM((cache, kv), bf16),
            pltpu.VMEM(cache_rope.shape[1:], bf16),
            pltpu.VMEM((cache, heads), f32),
            pltpu.VMEM((heads, kv), f32),
            pltpu.VMEM((experts * capacity, hidden), f32),
            pltpu.VMEM((experts * capacity, hidden), f32),
            pltpu.VMEM((experts * capacity, tokens), bf16),
            pltpu.VMEM((tokens, experts * capacity), bf16),
            pltpu.SemaphoreType.DMA((3, chunks)),
            pltpu.SemaphoreType.DMA((2,)),
            pltpu.SemaphoreType.DMA((chunks, nz + 2)),
            pltpu.SemaphoreType.DMA((chunks, nz + 2)),
            pltpu.SemaphoreType.DMA((chunks, nz + 2)),
            pltpu.SemaphoreType.DMA((chunks, nz + 2)),
        ],
        compiler_params=pltpu.CompilerParams(
            collective_id=0, has_side_effects=True, vmem_limit_bytes=VMEM_BYTES
        ),
        name="fused_moe_attention",
    )(
        moe_in,
        jnp.transpose(route_ids),
        jnp.transpose(route_weights),
        lengths,
        jnp.transpose(queries, (0, 2, 1)),
        w_gate,
        w_up,
        w_down,
        cache_latent,
        cache_rope,
    )
    return moe_out, attn_out


def solution(mesh):
    placed = (
        P(("node", "local"), None),
        P(("node", "local"), None),
        P(("node", "local"), None),
        P(("node", "local"), None, None),
        P(("node", "local"), None, None),
        P(("node", "local"), None, None),
        P(("node", "local"), None, None),
        P(("node", "local"), None, None),
        P(("node", "local"), None, None),
        P(("node", "local")),
    )
    if mesh.shape["node"] == 8 and mesh.shape["local"] == 4:
        local = functools.partial(local_fused, (2, 2, 2, 4))
    else:
        local = local_general
    return jax.shard_map(
        local,
        mesh=mesh,
        in_specs=placed,
        out_specs=(P(("node", "local"), None), P(("node", "local"), None, None)),
        check_vma=False,
    )
```

```python
import functools

import jax
import jax.numpy as jnp
from jax import lax
from jax.experimental import pallas as pl
from jax.experimental.pallas import tpu as pltpu
from jax.sharding import PartitionSpec as P

score_scale = 192.0 ** (-0.5)
MESH = pl.DeviceIdType.MESH
ROUTE_LANES = 128
ATT_PIECES = 4
IN_STEPS = 7
OUT_LAGS = (0, 2, 4, 6, 8)
IN_LAG = 2
CHUNKS = 7
VMEM_BYTES = 60 * 1024 * 1024


def expert_block(block, gate_one, up_one, down_one):
    model_width = block.shape[-1]
    rows_flat = block.reshape(-1, model_width)
    gate_act = jnp.dot(rows_flat, gate_one, preferred_element_type=jnp.float32)
    up_act = jnp.dot(rows_flat, up_one, preferred_element_type=jnp.float32)
    hidden_act = (jax.nn.silu(gate_act) * up_act).astype(jnp.bfloat16)
    result = jnp.dot(hidden_act, down_one, preferred_element_type=jnp.float32).astype(jnp.bfloat16)
    return result.reshape(block.shape)


def attention(queries, cache_latent, cache_rope, lengths):
    kv_width = cache_latent.shape[-1]
    scores = jnp.einsum(
        "rhc,rkc->rhk", queries[:, :, :kv_width], cache_latent, preferred_element_type=jnp.float32
    )
    scores = (
        scores
        + jnp.einsum(
            "rhc,rck->rhk", queries[:, :, kv_width:], cache_rope, preferred_element_type=jnp.float32
        )
    ) * score_scale
    positions = jnp.arange(cache_latent.shape[1], dtype=jnp.int32)
    scores = jnp.where(positions[None, None, :] < lengths[:, None, None], scores, -jnp.inf)
    peak = jnp.max(scores, axis=-1, keepdims=True)
    weights = jnp.exp(scores - peak)
    probs = (weights / jnp.sum(weights, axis=-1, keepdims=True)).astype(jnp.bfloat16)
    return jnp.einsum(
        "rhk,rkc->rhc", probs, cache_latent, preferred_element_type=jnp.float32
    ).astype(jnp.bfloat16)


def local_general(
    moe_in,
    route_ids,
    route_weights,
    w_gate,
    w_up,
    w_down,
    queries,
    cache_latent,
    cache_rope,
    lengths,
):
    attn_out = attention(queries, cache_latent, cache_rope, lengths)
    expert_count = lax.axis_size("node") * lax.axis_size("local")
    row_count, model_width = moe_in.shape
    top_count = route_ids.shape[1]
    capacity = 2 * row_count * top_count // expert_count
    row_index = jnp.broadcast_to(jnp.arange(row_count, dtype=jnp.int32)[:, None], route_ids.shape)
    padded = jnp.concatenate([moe_in, jnp.zeros((1, model_width), moe_in.dtype)], axis=0)
    expert_hits = (
        route_ids[:, :, None] == jnp.arange(expert_count, dtype=jnp.int32)[None, None, :]
    ).astype(jnp.int32)
    present = jnp.sum(expert_hits, axis=1, dtype=jnp.int32)
    earlier = jnp.cumsum(present, axis=0, dtype=jnp.int32) - present
    rank_of = jnp.sum(expert_hits * earlier[:, None, :], axis=-1, dtype=jnp.int32)
    slot_of = route_ids * capacity + rank_of
    table = (
        jnp.full((expert_count * capacity,), row_count, jnp.int32)
        .at[slot_of.reshape(-1)]
        .set(row_index.reshape(-1))
    )
    outgoing = padded[table].reshape(expert_count, capacity, model_width)
    result = expert_block(
        lax.all_to_all(outgoing, ("node", "local"), split_axis=0, concat_axis=0, tiled=True),
        w_gate[0],
        w_up[0],
        w_down[0],
    )
    returned = lax.all_to_all(result, ("node", "local"), split_axis=0, concat_axis=0, tiled=True)
    picked = returned.reshape(expert_count * capacity, model_width)[slot_of]
    total = jnp.einsum("rk,rkd->rd", route_weights, picked.astype(jnp.float32))
    return (total.astype(jnp.bfloat16), attn_out)


def fused_kernel(
    dims,
    capacity,
    x_ref,
    ids_ref,
    rw_ref,
    len_ref,
    q_ref,
    gate_hbm,
    up_hbm,
    down_hbm,
    latent_hbm,
    rope_hbm,
    moe_ref,
    attn_ref,
    gathered,
    part,
    recv_core,
    sum_core,
    recv_one,
    sum_one,
    recv_two,
    sum_two,
    recv_z,
    gate_w,
    up_w,
    down_w,
    latent,
    rope,
    scores,
    attn_acc,
    gate_acc,
    up_acc,
    pick,
    spread,
    load_sem,
    cache_sem,
    ag_send,
    ag_recv,
    rs_send,
    rs_recv,
):
    ny, nx, nc, nz = dims
    rows, width = x_ref.shape
    chunks = len(gathered)
    cw = width // chunks
    merge = chunks // IN_STEPS
    tokens = ny * nx * nc * nz * rows
    slots_total = ny * nx * nc * nz * capacity
    hidden = gate_w.shape[1]
    f32, bf16 = jnp.float32, jnp.bfloat16

    node = lax.axis_index("node")
    z = lax.axis_index("local")
    core = lax.rem(node, nc)
    x = lax.rem(node // nc, nx)
    y = node // (nc * nx)
    me = node * nz + z

    def device(yy, xx, cc, zz):
        return ((yy * nx + xx) * nc + cc, zz)

    p = y + core * (x - y)
    q = x + core * (y - x)
    core_dev = device(y, x, 1 - core, z)
    p_dev = device(y + (1 - core) * (1 - 2 * y), x + core * (1 - 2 * x), core, z)
    q_dev = device(y + core * (1 - 2 * y), x + (1 - core) * (1 - 2 * x), core, z)
    z_at = [lax.rem(z + o, nz) for o in range(nz)]
    z_devs = [device(y, x, core, z_at[o]) for o in range(1, nz)]

    barrier = pltpu.get_barrier_semaphore()
    for dev in [core_dev, p_dev, q_dev] + z_devs:
        pl.semaphore_signal(barrier, inc=1, device_id=dev, device_id_type=MESH)

    cache_loads = [
        pltpu.make_async_copy(latent_hbm.at[0], latent, cache_sem.at[0]),
        pltpu.make_async_copy(rope_hbm.at[0], rope, cache_sem.at[1]),
    ]
    for load in cache_loads:
        load.start()
    gate_loads, up_loads, down_loads = [], [], []
    for m in range(chunks // merge):
        at = pl.ds(m * merge * cw, merge * cw)
        gate_loads.append(
            pltpu.make_async_copy(gate_hbm.at[0, at], gate_w.at[at], load_sem.at[0, m])
        )
        up_loads.append(pltpu.make_async_copy(up_hbm.at[0, at], up_w.at[at], load_sem.at[1, m]))
    for c in range(chunks):
        at = pl.ds(c * cw, cw)
        down_loads.append(
            pltpu.make_async_copy(down_hbm.at[0, :, at], down_w.at[c], load_sem.at[2, c])
        )
    for m in range(chunks // merge):
        gate_loads[m].start()
        up_loads[m].start()
    for c in range(chunks):
        down_loads[c].start()

    lanes = lax.broadcasted_iota(jnp.int32, (rows, ROUTE_LANES), 1)
    ids = jnp.transpose(ids_ref[...])
    rw = jnp.transpose(rw_ref[...])
    table = jnp.zeros((rows, ROUTE_LANES), f32)
    for k in range(ids.shape[1]):
        table = table + jnp.where(lanes == ids[:, k : k + 1], rw[:, k : k + 1], 0.0)
    gathered[0][core, p, q, z, :, :ROUTE_LANES] = table.astype(bf16)
    gathered[0][core, p, q, z, :, ROUTE_LANES:] = x_ref[:, :cw]
    for c in range(1, chunks):
        gathered[c][core, p, q, z] = x_ref[:, c * cw : (c + 1) * cw]

    pl.semaphore_wait(barrier, 2 + nz)

    sends = []

    def push(src, dst, send_sem, recv_sem, dev):
        copy = pltpu.make_async_remote_copy(
            src_ref=src,
            dst_ref=dst,
            send_sem=send_sem,
            recv_sem=recv_sem,
            device_id=dev,
            device_id_type=MESH,
        )
        copy.start()
        sends.append(copy)

    def arrived(dst, send_sem, recv_sem, dev):
        pltpu.make_async_remote_copy(
            src_ref=dst,
            dst_ref=dst,
            send_sem=send_sem,
            recv_sem=recv_sem,
            device_id=dev,
            device_id_type=MESH,
        ).wait_recv()

    def gather_z(c):
        own = gathered[c].at[core, p, q, z]
        for o in range(1, nz):
            push(own, own, ag_send.at[c, o - 1], ag_recv.at[c, o - 1], z_devs[o - 1])

    def gather_z_wait(c):
        for o in range(1, nz):
            arrived(
                gathered[c].at[core, p, q, z_at[nz - o]],
                ag_send.at[c, o - 1],
                ag_recv.at[c, o - 1],
                z_devs[nz - o - 1],
            )

    def gather_views(c):
        g = gathered[c]
        return [
            (g.at[core, p, q], g.at[core, p, 1 - q], q_dev),
            (g.at[core, p], g.at[core, 1 - p], p_dev),
            (g.at[core], g.at[1 - core], core_dev),
        ]

    def gather_push(c, phase):
        src, _, dev = gather_views(c)[phase]
        k = nz - 1 + phase
        push(src, src, ag_send.at[c, k], ag_recv.at[c, k], dev)

    def gather_wait(c, phase):
        _, dst, dev = gather_views(c)[phase]
        k = nz - 1 + phase
        arrived(dst, ag_send.at[c, k], ag_recv.at[c, k], dev)

    kv = latent.shape[1]
    cache = latent.shape[0]
    piece = cache // ATT_PIECES
    length = len_ref[0]

    def score_piece(i):
        at = slice(i * piece, (i + 1) * piece)
        s = jnp.dot(latent[at, :], q_ref[0, :kv, :], preferred_element_type=f32)
        s = s + lax.dot_general(
            rope[:, at], q_ref[0, kv:, :], (((0,), (0,)), ((), ())), preferred_element_type=f32
        )
        positions = lax.broadcasted_iota(jnp.int32, s.shape, 0) + i * piece
        scores[at, :] = jnp.where(positions < length, s * score_scale, -jnp.inf)

    def soft():
        s = scores[...]
        e = jnp.exp(s - jnp.max(s, axis=0, keepdims=True))
        scores[...] = e / jnp.sum(e, axis=0, keepdims=True)

    def value_piece(i):
        at = slice(i * piece, (i + 1) * piece)
        got = lax.dot_general(
            scores[at, :].astype(bf16),
            latent[at, :],
            (((0,), (0,)), ((), ())),
            preferred_element_type=f32,
        )
        if i == 0:
            attn_acc[...] = got
        elif i < ATT_PIECES - 1:
            attn_acc[...] += got
        else:
            attn_ref[0] = (attn_acc[...] + got).astype(bf16)

    def first_piece():
        for load in cache_loads:
            load.wait()
        score_piece(0)

    tasks = [first_piece]
    tasks += [functools.partial(score_piece, i) for i in range(1, ATT_PIECES)]
    tasks += [soft]
    tasks += [functools.partial(value_piece, i) for i in range(ATT_PIECES)]

    def route():
        sent = gathered[0][:, :, :, :, :, :ROUTE_LANES].reshape(tokens, ROUTE_LANES)
        mine = (lax.broadcasted_iota(jnp.int32, (16, ROUTE_LANES), 1) == me).astype(bf16)
        weight = lax.dot_general(
            mine, sent, (((1,), (1,)), ((), ())), preferred_element_type=f32
        )
        present = weight > 0.0
        t_from = lax.broadcasted_iota(jnp.int32, (tokens, tokens), 0)
        t_to = lax.broadcasted_iota(jnp.int32, (tokens, tokens), 1)
        before = ((t_from < t_to) & (t_from // rows == t_to // rows)).astype(bf16)
        rank = jnp.dot(present.astype(bf16), before, preferred_element_type=f32)
        base = (lax.broadcasted_iota(jnp.int32, (16, tokens), 1) // rows) * capacity
        slot = jnp.where(present, rank + base.astype(f32), -1.0)
        slot_id = lax.broadcasted_iota(jnp.int32, (slots_total, tokens), 0).astype(f32)
        hit = slot[0:1, :] == slot_id
        pick[...] = hit.astype(bf16)
        spread[...] = jnp.transpose(jnp.where(hit, weight[0:1, :], 0.0)).astype(bf16)

    def expert_in(m):
        picked = []
        for c in range(m * merge, (m + 1) * merge):
            g = gathered[c][...] if c else gathered[c][:, :, :, :, :, ROUTE_LANES:]
            picked.append(
                jnp.dot(pick[...], g.reshape(tokens, cw), preferred_element_type=f32).astype(bf16)
            )
        rows_in = picked[0] if merge == 1 else jnp.concatenate(picked, axis=1)
        gate_loads[m].wait()
        up_loads[m].wait()
        at = slice(m * merge * cw, (m + 1) * merge * cw)
        for acc, w in ((gate_acc, gate_w), (up_acc, up_w)):
            got = jnp.dot(rows_in, w[at, :], preferred_element_type=f32)
            if m == 0:
                acc[...] = got
            else:
                acc[...] += got

    for c in range(chunks):
        gather_z(c)
    for s in range(chunks + 3 * IN_LAG):
        if s < chunks:
            gather_z_wait(s)
            gather_push(s, 0)
        for phase in range(2):
            c = s - IN_LAG * (1 + phase)
            if 0 <= c < chunks:
                gather_wait(c, phase)
                gather_push(c, phase + 1)
        for _ in range(2 if s < 3 else 1):
            if tasks:
                tasks.pop(0)()
        c = s - 3 * IN_LAG
        if 0 <= c < chunks:
            gather_wait(c, 2)
            if c == 0:
                route()
            if c % merge == merge - 1:
                expert_in(c // merge)
    for task in tasks:
        task()

    gate = gate_acc[...]
    hidden_act = (gate / (1.0 + jnp.exp(-gate)) * up_acc[...]).astype(bf16)

    def add_to(dst, a, b):
        dst[...] = (a.astype(f32) + b.astype(f32)).astype(bf16)

    def out_views(c):
        return [
            (part[c].at[1 - core], recv_core[c], core_dev),
            (sum_core[c].at[1 - p], recv_one[c], p_dev),
            (sum_one[c].at[1 - q], recv_two[c], q_dev),
        ]

    def out_push(c, phase):
        src, dst, dev = out_views(c)[phase]
        push(src, dst, rs_send.at[c, phase], rs_recv.at[c, phase], dev)

    def out_wait(c, phase):
        _, dst, dev = out_views(c)[phase]
        arrived(dst, rs_send.at[c, phase], rs_recv.at[c, phase], dev)

    def stage_zero(c):
        down_loads[c].wait()
        out = jnp.dot(hidden_act, down_w[c], preferred_element_type=f32).astype(bf16)
        got = jnp.dot(spread[...], out, preferred_element_type=f32).astype(bf16)
        part[c][...] = got.reshape(part[c].shape)
        out_push(c, 0)

    def stage_one(c):
        out_wait(c, 0)
        add_to(sum_core[c], part[c][core], recv_core[c][...])
        out_push(c, 1)

    def stage_two(c):
        out_wait(c, 1)
        add_to(sum_one[c], sum_core[c][p], recv_one[c][...])
        out_push(c, 2)

    def stage_three(c):
        out_wait(c, 2)
        add_to(sum_two[c], sum_one[c][q], recv_two[c][...])
        for o in range(1, nz):
            push(
                sum_two[c].at[z_at[o]],
                recv_z[c].at[o - 1],
                rs_send.at[c, 2 + o],
                rs_recv.at[c, 2 + o],
                z_devs[o - 1],
            )

    def stage_four(c):
        total = sum_two[c][z].astype(f32)
        for o in range(1, nz):
            arrived(
                recv_z[c].at[o - 1], rs_send.at[c, 2 + o], rs_recv.at[c, 2 + o], z_devs[nz - o - 1]
            )
            total = total + recv_z[c][o - 1].astype(f32)
        moe_ref[:, c * cw : (c + 1) * cw] = total.astype(bf16)

    stages = [stage_zero, stage_one, stage_two, stage_three, stage_four]
    for s in range(chunks + OUT_LAGS[-1]):
        for lag, stage in zip(OUT_LAGS, stages):
            c = s - lag
            if 0 <= c < chunks:
                stage(c)

    for copy in sends:
        copy.wait_send()


def local_fused(
    dims,
    moe_in,
    route_ids,
    route_weights,
    w_gate,
    w_up,
    w_down,
    queries,
    cache_latent,
    cache_rope,
    lengths,
):
    ny, nx, nc, nz = dims
    experts = ny * nx * nc * nz
    rows, width = moe_in.shape
    capacity = 2 * rows * route_ids.shape[1] // experts
    hidden = w_gate.shape[2]
    cache, kv = cache_latent.shape[1:]
    heads = queries.shape[1]
    tokens = experts * rows
    chunks = CHUNKS
    cw = width // chunks
    bf16, f32 = jnp.bfloat16, jnp.float32

    def each(shape, extra=0):
        return [
            pltpu.VMEM(shape + (cw + (extra if c == 0 else 0),), bf16) for c in range(chunks)
        ]

    vmem = pl.BlockSpec(memory_space=pltpu.VMEM)
    hbm = pl.BlockSpec(memory_space=pl.ANY)
    moe_out, attn_out = pl.pallas_call(
        functools.partial(fused_kernel, dims, capacity),
        out_shape=(
            jax.ShapeDtypeStruct((rows, width), bf16),
            jax.ShapeDtypeStruct((1, heads, kv), bf16),
        ),
        in_specs=[
            vmem,
            vmem,
            vmem,
            pl.BlockSpec(memory_space=pltpu.SMEM),
            vmem,
            hbm,
            hbm,
            hbm,
            hbm,
            hbm,
        ],
        out_specs=(vmem, vmem),
        scratch_shapes=[
            each((nc, 2, 2, nz, rows), ROUTE_LANES),
            each((nc, 2, 2, nz, rows)),
            each((2, 2, nz, rows)),
            each((2, 2, nz, rows)),
            each((2, nz, rows)),
            each((2, nz, rows)),
            each((nz, rows)),
            each((nz, rows)),
            each((nz - 1, rows)),
            pltpu.VMEM((width, hidden), bf16),
            pltpu.VMEM((width, hidden), bf16),
            pltpu.VMEM((chunks, hidden, cw), bf16),
            pltpu.VMEM((cache, kv), bf16),
            pltpu.VMEM(cache_rope.shape[1:], bf16),
            pltpu.VMEM((cache, heads), f32),
            pltpu.VMEM((heads, kv), f32),
            pltpu.VMEM((experts * capacity, hidden), f32),
            pltpu.VMEM((experts * capacity, hidden), f32),
            pltpu.VMEM((experts * capacity, tokens), bf16),
            pltpu.VMEM((tokens, experts * capacity), bf16),
            pltpu.SemaphoreType.DMA((3, chunks)),
            pltpu.SemaphoreType.DMA((2,)),
            pltpu.SemaphoreType.DMA((chunks, nz + 2)),
            pltpu.SemaphoreType.DMA((chunks, nz + 2)),
            pltpu.SemaphoreType.DMA((chunks, nz + 2)),
            pltpu.SemaphoreType.DMA((chunks, nz + 2)),
        ],
        compiler_params=pltpu.CompilerParams(
            collective_id=0, has_side_effects=True, vmem_limit_bytes=VMEM_BYTES
        ),
        name="fused_moe_attention",
    )(
        moe_in,
        jnp.transpose(route_ids),
        jnp.transpose(route_weights),
        lengths,
        jnp.transpose(queries, (0, 2, 1)),
        w_gate,
        w_up,
        w_down,
        cache_latent,
        cache_rope,
    )
    return moe_out, attn_out


def solution(mesh):
    placed = (
        P(("node", "local"), None),
        P(("node", "local"), None),
        P(("node", "local"), None),
        P(("node", "local"), None, None),
        P(("node", "local"), None, None),
        P(("node", "local"), None, None),
        P(("node", "local"), None, None),
        P(("node", "local"), None, None),
        P(("node", "local"), None, None),
        P(("node", "local")),
    )
    if mesh.shape["node"] == 8 and mesh.shape["local"] == 4:
        local = functools.partial(local_fused, (2, 2, 2, 4))
    else:
        local = local_general
    return jax.shard_map(
        local,
        mesh=mesh,
        in_specs=placed,
        out_specs=(P(("node", "local"), None), P(("node", "local"), None, None)),
        check_vma=False,
    )
```

```python
import functools

import jax
import jax.numpy as jnp
from jax import lax
from jax.experimental import pallas as pl
from jax.experimental.pallas import tpu as pltpu
from jax.sharding import PartitionSpec as P

score_scale = 192.0 ** (-0.5)
MESH = pl.DeviceIdType.MESH
ROUTE_LANES = 128
ATT_PIECES = 4
IN_STEPS = 7
OUT_LAGS = (0, 2, 4, 6, 8)
IN_LAG = 2
CHUNKS = 14
VMEM_BYTES = 60 * 1024 * 1024


def expert_block(block, gate_one, up_one, down_one):
    model_width = block.shape[-1]
    rows_flat = block.reshape(-1, model_width)
    gate_act = jnp.dot(rows_flat, gate_one, preferred_element_type=jnp.float32)
    up_act = jnp.dot(rows_flat, up_one, preferred_element_type=jnp.float32)
    hidden_act = (jax.nn.silu(gate_act) * up_act).astype(jnp.bfloat16)
    result = jnp.dot(hidden_act, down_one, preferred_element_type=jnp.float32).astype(jnp.bfloat16)
    return result.reshape(block.shape)


def attention(queries, cache_latent, cache_rope, lengths):
    kv_width = cache_latent.shape[-1]
    scores = jnp.einsum(
        "rhc,rkc->rhk", queries[:, :, :kv_width], cache_latent, preferred_element_type=jnp.float32
    )
    scores = (
        scores
        + jnp.einsum(
            "rhc,rck->rhk", queries[:, :, kv_width:], cache_rope, preferred_element_type=jnp.float32
        )
    ) * score_scale
    positions = jnp.arange(cache_latent.shape[1], dtype=jnp.int32)
    scores = jnp.where(positions[None, None, :] < lengths[:, None, None], scores, -jnp.inf)
    peak = jnp.max(scores, axis=-1, keepdims=True)
    weights = jnp.exp(scores - peak)
    probs = (weights / jnp.sum(weights, axis=-1, keepdims=True)).astype(jnp.bfloat16)
    return jnp.einsum(
        "rhk,rkc->rhc", probs, cache_latent, preferred_element_type=jnp.float32
    ).astype(jnp.bfloat16)


def local_general(
    moe_in,
    route_ids,
    route_weights,
    w_gate,
    w_up,
    w_down,
    queries,
    cache_latent,
    cache_rope,
    lengths,
):
    attn_out = attention(queries, cache_latent, cache_rope, lengths)
    expert_count = lax.axis_size("node") * lax.axis_size("local")
    row_count, model_width = moe_in.shape
    top_count = route_ids.shape[1]
    capacity = 2 * row_count * top_count // expert_count
    row_index = jnp.broadcast_to(jnp.arange(row_count, dtype=jnp.int32)[:, None], route_ids.shape)
    padded = jnp.concatenate([moe_in, jnp.zeros((1, model_width), moe_in.dtype)], axis=0)
    expert_hits = (
        route_ids[:, :, None] == jnp.arange(expert_count, dtype=jnp.int32)[None, None, :]
    ).astype(jnp.int32)
    present = jnp.sum(expert_hits, axis=1, dtype=jnp.int32)
    earlier = jnp.cumsum(present, axis=0, dtype=jnp.int32) - present
    rank_of = jnp.sum(expert_hits * earlier[:, None, :], axis=-1, dtype=jnp.int32)
    slot_of = route_ids * capacity + rank_of
    table = (
        jnp.full((expert_count * capacity,), row_count, jnp.int32)
        .at[slot_of.reshape(-1)]
        .set(row_index.reshape(-1))
    )
    outgoing = padded[table].reshape(expert_count, capacity, model_width)
    result = expert_block(
        lax.all_to_all(outgoing, ("node", "local"), split_axis=0, concat_axis=0, tiled=True),
        w_gate[0],
        w_up[0],
        w_down[0],
    )
    returned = lax.all_to_all(result, ("node", "local"), split_axis=0, concat_axis=0, tiled=True)
    picked = returned.reshape(expert_count * capacity, model_width)[slot_of]
    total = jnp.einsum("rk,rkd->rd", route_weights, picked.astype(jnp.float32))
    return (total.astype(jnp.bfloat16), attn_out)


def fused_kernel(
    dims,
    capacity,
    x_ref,
    ids_ref,
    rw_ref,
    len_ref,
    q_ref,
    gate_hbm,
    up_hbm,
    down_hbm,
    latent_hbm,
    rope_hbm,
    moe_ref,
    attn_ref,
    gathered,
    part,
    recv_core,
    sum_core,
    recv_one,
    sum_one,
    recv_two,
    sum_two,
    recv_z,
    gate_w,
    up_w,
    down_w,
    latent,
    rope,
    scores,
    attn_acc,
    gate_acc,
    up_acc,
    pick,
    spread,
    before,
    load_sem,
    cache_sem,
    ag_send,
    ag_recv,
    rs_send,
    rs_recv,
):
    ny, nx, nc, nz = dims
    rows, width = x_ref.shape
    chunks = len(gathered)
    cw = width // chunks
    merge = chunks // IN_STEPS
    tokens = ny * nx * nc * nz * rows
    slots_total = ny * nx * nc * nz * capacity
    hidden = gate_w.shape[1]
    f32, bf16 = jnp.float32, jnp.bfloat16

    node = lax.axis_index("node")
    z = lax.axis_index("local")
    core = lax.rem(node, nc)
    x = lax.rem(node // nc, nx)
    y = node // (nc * nx)
    me = node * nz + z

    def device(yy, xx, cc, zz):
        return ((yy * nx + xx) * nc + cc, zz)

    p = y + core * (x - y)
    q = x + core * (y - x)
    core_dev = device(y, x, 1 - core, z)
    p_dev = device(y + (1 - core) * (1 - 2 * y), x + core * (1 - 2 * x), core, z)
    q_dev = device(y + core * (1 - 2 * y), x + (1 - core) * (1 - 2 * x), core, z)
    z_at = [lax.rem(z + o, nz) for o in range(nz)]
    z_devs = [device(y, x, core, z_at[o]) for o in range(1, nz)]

    barrier = pltpu.get_barrier_semaphore()
    for dev in [core_dev, p_dev, q_dev] + z_devs:
        pl.semaphore_signal(barrier, inc=1, device_id=dev, device_id_type=MESH)

    cache_loads = [
        pltpu.make_async_copy(latent_hbm.at[0], latent, cache_sem.at[0]),
        pltpu.make_async_copy(rope_hbm.at[0], rope, cache_sem.at[1]),
    ]
    for load in cache_loads:
        load.start()
    gate_loads, up_loads, down_loads = [], [], []
    for m in range(chunks // merge):
        at = pl.ds(m * merge * cw, merge * cw)
        gate_loads.append(
            pltpu.make_async_copy(gate_hbm.at[0, at], gate_w.at[at], load_sem.at[0, m])
        )
        up_loads.append(pltpu.make_async_copy(up_hbm.at[0, at], up_w.at[at], load_sem.at[1, m]))
    for c in range(chunks):
        at = pl.ds(c * cw, cw)
        down_loads.append(
            pltpu.make_async_copy(down_hbm.at[0, :, at], down_w.at[c], load_sem.at[2, c])
        )
    for m in range(chunks // merge):
        gate_loads[m].start()
        up_loads[m].start()
    for c in range(chunks):
        down_loads[c].start()

    lanes = lax.broadcasted_iota(jnp.int32, (rows, ROUTE_LANES), 1)
    ids = jnp.transpose(ids_ref[...])
    rw = jnp.transpose(rw_ref[...])
    table = jnp.zeros((rows, ROUTE_LANES), f32)
    for k in range(ids.shape[1]):
        table = table + jnp.where(lanes == ids[:, k : k + 1], rw[:, k : k + 1], 0.0)
    gathered[0][core, p, q, z, :, :ROUTE_LANES] = table.astype(bf16)
    gathered[0][core, p, q, z, :, ROUTE_LANES:] = x_ref[:, :cw]
    for c in range(1, chunks):
        gathered[c][core, p, q, z] = x_ref[:, c * cw : (c + 1) * cw]

    t_from = lax.broadcasted_iota(jnp.int32, (tokens, tokens), 0)
    t_to = lax.broadcasted_iota(jnp.int32, (tokens, tokens), 1)
    before[...] = ((t_from < t_to) & (t_from // rows == t_to // rows)).astype(bf16)

    pl.semaphore_wait(barrier, 2 + nz)

    sends = []

    def push(src, dst, send_sem, recv_sem, dev):
        copy = pltpu.make_async_remote_copy(
            src_ref=src,
            dst_ref=dst,
            send_sem=send_sem,
            recv_sem=recv_sem,
            device_id=dev,
            device_id_type=MESH,
        )
        copy.start()
        sends.append(copy)

    def arrived(dst, send_sem, recv_sem, dev):
        pltpu.make_async_remote_copy(
            src_ref=dst,
            dst_ref=dst,
            send_sem=send_sem,
            recv_sem=recv_sem,
            device_id=dev,
            device_id_type=MESH,
        ).wait_recv()

    def gather_z(c):
        own = gathered[c].at[core, p, q, z]
        for o in range(1, nz):
            push(own, own, ag_send.at[c, o - 1], ag_recv.at[c, o - 1], z_devs[o - 1])

    def gather_z_wait(c):
        for o in range(1, nz):
            arrived(
                gathered[c].at[core, p, q, z_at[nz - o]],
                ag_send.at[c, o - 1],
                ag_recv.at[c, o - 1],
                z_devs[nz - o - 1],
            )

    def gather_views(c):
        g = gathered[c]
        return [
            (g.at[core, p, q], g.at[core, p, 1 - q], q_dev),
            (g.at[core, p], g.at[core, 1 - p], p_dev),
            (g.at[core], g.at[1 - core], core_dev),
        ]

    def gather_push(c, phase):
        src, _, dev = gather_views(c)[phase]
        k = nz - 1 + phase
        push(src, src, ag_send.at[c, k], ag_recv.at[c, k], dev)

    def gather_wait(c, phase):
        _, dst, dev = gather_views(c)[phase]
        k = nz - 1 + phase
        arrived(dst, ag_send.at[c, k], ag_recv.at[c, k], dev)

    kv = latent.shape[1]
    cache = latent.shape[0]
    piece = cache // ATT_PIECES
    length = len_ref[0]

    def score_piece(i):
        at = slice(i * piece, (i + 1) * piece)
        s = jnp.dot(latent[at, :], q_ref[0, :kv, :], preferred_element_type=f32)
        s = s + lax.dot_general(
            rope[:, at], q_ref[0, kv:, :], (((0,), (0,)), ((), ())), preferred_element_type=f32
        )
        positions = lax.broadcasted_iota(jnp.int32, s.shape, 0) + i * piece
        scores[at, :] = jnp.where(positions < length, s * score_scale, -jnp.inf)

    def soft():
        s = scores[...]
        e = jnp.exp(s - jnp.max(s, axis=0, keepdims=True))
        scores[...] = e / jnp.sum(e, axis=0, keepdims=True)

    def value_piece(i):
        at = slice(i * piece, (i + 1) * piece)
        got = lax.dot_general(
            scores[at, :].astype(bf16),
            latent[at, :],
            (((0,), (0,)), ((), ())),
            preferred_element_type=f32,
        )
        if i == 0:
            attn_acc[...] = got
        elif i < ATT_PIECES - 1:
            attn_acc[...] += got
        else:
            attn_ref[0] = (attn_acc[...] + got).astype(bf16)

    def first_piece():
        for load in cache_loads:
            load.wait()
        score_piece(0)

    tasks = [first_piece]
    tasks += [functools.partial(score_piece, i) for i in range(1, ATT_PIECES)]
    tasks += [soft]
    tasks += [functools.partial(value_piece, i) for i in range(ATT_PIECES)]

    def route():
        sent = gathered[0][:, :, :, :, :, :ROUTE_LANES].reshape(tokens, ROUTE_LANES)
        mine = (lax.broadcasted_iota(jnp.int32, (16, ROUTE_LANES), 1) == me).astype(bf16)
        weight = lax.dot_general(
            mine, sent, (((1,), (1,)), ((), ())), preferred_element_type=f32
        )
        present = weight > 0.0
        rank = jnp.dot(present.astype(bf16), before[...], preferred_element_type=f32)
        base = (lax.broadcasted_iota(jnp.int32, (16, tokens), 1) // rows) * capacity
        slot = jnp.where(present, rank + base.astype(f32), -1.0)
        slot_id = lax.broadcasted_iota(jnp.int32, (slots_total, tokens), 0).astype(f32)
        hit = slot[0:1, :] == slot_id
        pick[...] = hit.astype(bf16)
        spread[...] = jnp.transpose(jnp.where(hit, weight[0:1, :], 0.0)).astype(bf16)

    def expert_in(m):
        picked = []
        for c in range(m * merge, (m + 1) * merge):
            g = gathered[c][...] if c else gathered[c][:, :, :, :, :, ROUTE_LANES:]
            picked.append(
                jnp.dot(pick[...], g.reshape(tokens, cw), preferred_element_type=f32).astype(bf16)
            )
        rows_in = picked[0] if merge == 1 else jnp.concatenate(picked, axis=1)
        gate_loads[m].wait()
        up_loads[m].wait()
        at = slice(m * merge * cw, (m + 1) * merge * cw)
        for acc, w in ((gate_acc, gate_w), (up_acc, up_w)):
            got = jnp.dot(rows_in, w[at, :], preferred_element_type=f32)
            if m == 0:
                acc[...] = got
            else:
                acc[...] += got

    for c in range(chunks):
        gather_z(c)
    for s in range(chunks + 3 * IN_LAG):
        if s < chunks:
            gather_z_wait(s)
            gather_push(s, 0)
        for phase in range(2):
            c = s - IN_LAG * (1 + phase)
            if 0 <= c < chunks:
                gather_wait(c, phase)
                gather_push(c, phase + 1)
        for _ in range(2 if s < 3 else 1):
            if tasks:
                tasks.pop(0)()
        c = s - 3 * IN_LAG
        if 0 <= c < chunks:
            gather_wait(c, 2)
            if c == 0:
                route()
            if c % merge == merge - 1:
                expert_in(c // merge)
    for task in tasks:
        task()

    gate = gate_acc[...]
    hidden_act = (gate / (1.0 + jnp.exp(-gate)) * up_acc[...]).astype(bf16)

    def add_to(dst, a, b):
        dst[...] = (a.astype(f32) + b.astype(f32)).astype(bf16)

    def out_views(c):
        return [
            (part[c].at[1 - core], recv_core[c], core_dev),
            (sum_core[c].at[1 - p], recv_one[c], p_dev),
            (sum_one[c].at[1 - q], recv_two[c], q_dev),
        ]

    def out_push(c, phase):
        src, dst, dev = out_views(c)[phase]
        push(src, dst, rs_send.at[c, phase], rs_recv.at[c, phase], dev)

    def out_wait(c, phase):
        _, dst, dev = out_views(c)[phase]
        arrived(dst, rs_send.at[c, phase], rs_recv.at[c, phase], dev)

    def stage_zero(c):
        down_loads[c].wait()
        out = jnp.dot(hidden_act, down_w[c], preferred_element_type=f32).astype(bf16)
        got = jnp.dot(spread[...], out, preferred_element_type=f32).astype(bf16)
        part[c][...] = got.reshape(part[c].shape)
        out_push(c, 0)

    def stage_one(c):
        out_wait(c, 0)
        add_to(sum_core[c], part[c][core], recv_core[c][...])
        out_push(c, 1)

    def stage_two(c):
        out_wait(c, 1)
        add_to(sum_one[c], sum_core[c][p], recv_one[c][...])
        out_push(c, 2)

    def stage_three(c):
        out_wait(c, 2)
        add_to(sum_two[c], sum_one[c][q], recv_two[c][...])
        for o in range(1, nz):
            push(
                sum_two[c].at[z_at[o]],
                recv_z[c].at[o - 1],
                rs_send.at[c, 2 + o],
                rs_recv.at[c, 2 + o],
                z_devs[o - 1],
            )

    def stage_four(c):
        total = sum_two[c][z].astype(f32)
        for o in range(1, nz):
            arrived(
                recv_z[c].at[o - 1], rs_send.at[c, 2 + o], rs_recv.at[c, 2 + o], z_devs[nz - o - 1]
            )
            total = total + recv_z[c][o - 1].astype(f32)
        moe_ref[:, c * cw : (c + 1) * cw] = total.astype(bf16)

    stages = [stage_zero, stage_one, stage_two, stage_three, stage_four]
    for s in range(chunks + OUT_LAGS[-1]):
        for lag, stage in zip(OUT_LAGS, stages):
            c = s - lag
            if 0 <= c < chunks:
                stage(c)

    for copy in sends:
        copy.wait_send()


def local_fused(
    dims,
    moe_in,
    route_ids,
    route_weights,
    w_gate,
    w_up,
    w_down,
    queries,
    cache_latent,
    cache_rope,
    lengths,
):
    ny, nx, nc, nz = dims
    experts = ny * nx * nc * nz
    rows, width = moe_in.shape
    capacity = 2 * rows * route_ids.shape[1] // experts
    hidden = w_gate.shape[2]
    cache, kv = cache_latent.shape[1:]
    heads = queries.shape[1]
    tokens = experts * rows
    chunks = CHUNKS
    cw = width // chunks
    bf16, f32 = jnp.bfloat16, jnp.float32

    def each(shape, extra=0):
        return [
            pltpu.VMEM(shape + (cw + (extra if c == 0 else 0),), bf16) for c in range(chunks)
        ]

    vmem = pl.BlockSpec(memory_space=pltpu.VMEM)
    hbm = pl.BlockSpec(memory_space=pl.ANY)
    moe_out, attn_out = pl.pallas_call(
        functools.partial(fused_kernel, dims, capacity),
        out_shape=(
            jax.ShapeDtypeStruct((rows, width), bf16),
            jax.ShapeDtypeStruct((1, heads, kv), bf16),
        ),
        in_specs=[
            vmem,
            vmem,
            vmem,
            pl.BlockSpec(memory_space=pltpu.SMEM),
            vmem,
            hbm,
            hbm,
            hbm,
            hbm,
            hbm,
        ],
        out_specs=(vmem, vmem),
        scratch_shapes=[
            each((nc, 2, 2, nz, rows), ROUTE_LANES),
            each((nc, 2, 2, nz, rows)),
            each((2, 2, nz, rows)),
            each((2, 2, nz, rows)),
            each((2, nz, rows)),
            each((2, nz, rows)),
            each((nz, rows)),
            each((nz, rows)),
            each((nz - 1, rows)),
            pltpu.VMEM((width, hidden), bf16),
            pltpu.VMEM((width, hidden), bf16),
            pltpu.VMEM((chunks, hidden, cw), bf16),
            pltpu.VMEM((cache, kv), bf16),
            pltpu.VMEM(cache_rope.shape[1:], bf16),
            pltpu.VMEM((cache, heads), f32),
            pltpu.VMEM((heads, kv), f32),
            pltpu.VMEM((experts * capacity, hidden), f32),
            pltpu.VMEM((experts * capacity, hidden), f32),
            pltpu.VMEM((experts * capacity, tokens), bf16),
            pltpu.VMEM((tokens, experts * capacity), bf16),
            pltpu.VMEM((tokens, tokens), bf16),
            pltpu.SemaphoreType.DMA((3, chunks)),
            pltpu.SemaphoreType.DMA((2,)),
            pltpu.SemaphoreType.DMA((chunks, nz + 2)),
            pltpu.SemaphoreType.DMA((chunks, nz + 2)),
            pltpu.SemaphoreType.DMA((chunks, nz + 2)),
            pltpu.SemaphoreType.DMA((chunks, nz + 2)),
        ],
        compiler_params=pltpu.CompilerParams(
            collective_id=0, has_side_effects=True, vmem_limit_bytes=VMEM_BYTES
        ),
        name="fused_moe_attention",
    )(
        moe_in,
        jnp.transpose(route_ids),
        jnp.transpose(route_weights),
        lengths,
        jnp.transpose(queries, (0, 2, 1)),
        w_gate,
        w_up,
        w_down,
        cache_latent,
        cache_rope,
    )
    return moe_out, attn_out


def solution(mesh):
    placed = (
        P(("node", "local"), None),
        P(("node", "local"), None),
        P(("node", "local"), None),
        P(("node", "local"), None, None),
        P(("node", "local"), None, None),
        P(("node", "local"), None, None),
        P(("node", "local"), None, None),
        P(("node", "local"), None, None),
        P(("node", "local"), None, None),
        P(("node", "local")),
    )
    if mesh.shape["node"] == 8 and mesh.shape["local"] == 4:
        local = functools.partial(local_fused, (2, 2, 2, 4))
    else:
        local = local_general
    return jax.shard_map(
        local,
        mesh=mesh,
        in_specs=placed,
        out_specs=(P(("node", "local"), None), P(("node", "local"), None, None)),
        check_vma=False,
    )
```
